32 devices in a mesh: grp: 1, row: 8 (over z, y), col: 4 (over x, core).
Axes of the slice: x: 2, y: 2, z: 4, core: 2. Of those that a mesh axis runs over, the one named last changes fastest.
Arguments:
- pair_act: bfloat16 [128, 128, 128], P(('grp', 'row'), 'col'), may hold values from -6 to 6
- single: bfloat16 [128, 768], P(('grp', 'row')), may hold values from -6 to 6
- token_mask: int32 [128], P('grp'), may hold values from 0 to 1, as said below
- chain_index: int32 [128], P('grp'), may hold values from 0 to 7, never falling along the last dimension, each value on 1 to 32 neighbouring positions
- residue_index: int32 [128], P('grp'), may hold values from 1 to 192, as said below
- tri_gain: float32 [2, 128], replicated, may hold values from 0.25 to 1.75
- tri_qk: bfloat16 [2, 128, 256], replicated, may hold values from -1.5 to 1.5
- tri_vg: bfloat16 [2, 128, 256], replicated, may hold values from -0.5 to 0.5
- tri_out: bfloat16 [2, 128, 128], replicated, may hold values from -0.5 to 0.5
- bias_gain: float32 [128], replicated, may hold values from 0.25 to 1.75
- bias_proj: bfloat16 [128, 16], replicated, may hold values from -0.5 to 0.5
- chain_bias: float32 [16], P('col'), may hold values from -4 to 4
- pos_slope: float32 [16], P('col'), may hold values from -6 to 6
- attn_gain: float32 [768], replicated, may hold values from 0.25 to 1.75
- attn_qk: bfloat16 [2, 768, 768], P(None, None, 'col'), may hold values from -0.375 to 0.375
- attn_vg: bfloat16 [2, 768, 768], P(None, None, 'col'), may hold values from -0.21875 to 0.21875
- attn_out: bfloat16 [768, 768], P('col'), may hold values from -0.875 to 0.875
Outputs:
- pair_out: bfloat16 [128, 128, 128], P(('grp', 'row'), 'col')
- token_update: bfloat16 [128, 768], P(('grp', 'row'), 'col')
The draws below stay inside these ranges and needn't reach their ends.
Inputs may be any that keep to these rules, and one draw needn't show every extreme that they name: `token_mask`: 1 on a leading run of at least 64 positions, 0 on the rest, and some position is 0. `chain_index`: never decreasing along the positions; all 8 chains occur. `residue_index`: starts at 1 and rises by 1 or 2 from each position to the next, by 2 at exactly 64 of them.
All inputs are finite; a program needn't handle non-finite values.
Results may differ from the reference program's by a relative error of at most 0.019.
Values may be sent and summed in bfloat16 or wider, within the bound.
A program may use at most 64 MiB of HBM per device.

```python
import math
import jax
import jax.numpy as jnp
import numpy as np
from jax import lax

TOKENS = 128
C = 128
TRI_HEADS = 8
TRI_DIM = 16
D = 768
HEADS = 16
HEAD_DIM = 48
N_ROW = 8


def draw_token_mask(key, part):
    length = jax.random.randint(key, (), TOKENS // 2, TOKENS)
    return (jnp.arange(TOKENS) < length).astype(jnp.int32)


def draw_residue_index(key, part):
    order = jax.random.permutation(jax.random.fold_in(key, 7), TOKENS - 1)
    steps_drawn = jnp.where(order < TOKENS // 2, 2, 1).astype(jnp.int32)
    running_sum = jnp.concatenate([jnp.zeros((1,), jnp.int32), jnp.cumsum(steps_drawn).astype(jnp.int32)])
    return (running_sum + 1).astype(jnp.int32)


def levels(own_key, shape, cuts, smallest, high):
    level = 1.0
    for position, blocks in cuts:
        heights = jax.random.uniform(jax.random.fold_in(jax.random.fold_in(own_key, 6), position), (blocks,), jnp.float32, smallest / len(cuts), high / len(cuts))
        level = level * jnp.repeat(jnp.exp(heights), shape[position] // blocks).reshape((-1,) + (1,) * (len(shape) - 1 - position))
    return level


def length_profile(number_of, total, reach, lean):
    portions = [(1 << 20) // math.isqrt(rank ** lean) + 1 for rank in range(2, number_of + 1)]
    rest, holding = total - reach - (number_of - 1), [1] * (number_of - 1)
    while rest > 0:
        candidates = [i for i in range(number_of - 1) if holding[i] < reach]
        pool, left = sum([portions[i] for i in candidates]), rest
        for i in candidates:
            addition = min(reach - holding[i], max(1, left * portions[i] // pool), rest)
            holding[i] = holding[i] + addition
            rest = rest - addition
    return np.array([reach] + holding)


def ragged_sizes(own_key, count, total, most, skew):
    if count == 2:
        one = jax.random.randint(own_key, (), max(1, total - most), min(most, total - 1) + 1)
        return jnp.stack([one, total - one])
    lengths = jnp.asarray(length_profile(count, total, most, skew), jnp.int32)
    couples = (count - 1) // 2
    giver, sink = lengths[1:1 + 2 * couples:2], lengths[2:2 + 2 * couples:2]
    slack = jnp.minimum(giver - 1, most - sink)
    moved = jax.random.randint(jax.random.fold_in(own_key, 1), (couples,), 0, 1 << 20) % (slack + 1)
    lengths = lengths.at[1:1 + 2 * couples:2].set(giver - moved).at[2:2 + 2 * couples:2].set(sink + moved)
    return lengths[jax.random.permutation(jax.random.fold_in(own_key, 2), count)]


def gaussian(key, shape, width, reach, shards=(), kind=jnp.bfloat16):
    level = levels(key, shape, shards, -0.22, 0.18) if shards else 1.0
    entries = jax.random.normal(key, shape, jnp.float32) * width * level
    return jnp.minimum(jnp.maximum(entries, -reach), reach).astype(kind)


def setup_inputs(seed: int = 0, part: int = 0) -> dict:
    splits = jax.random.split(jax.random.key(seed), 18)
    own_keys = jax.random.split(jax.random.fold_in(splits[17], part), 18)
    pair_act = gaussian(own_keys[0], (TOKENS, TOKENS, C), 1.0, 6.0, ((0, 8), (1, 4)))
    single = gaussian(own_keys[1], (TOKENS, D), 1.0, 6.0, ((0, 8),))
    token_mask = draw_token_mask(jax.random.fold_in(jax.random.fold_in(splits[17], part), 71), part)
    chain_index = jnp.searchsorted(jnp.cumsum(ragged_sizes(own_keys[3], 8, TOKENS, TOKENS // 4, 0)), jnp.arange(TOKENS), side="right").astype(jnp.int32)
    residue_index = draw_residue_index(jax.random.fold_in(jax.random.fold_in(splits[17], part), 71), part)
    tri_gain = jnp.clip(1.0 + 0.15 * jax.random.normal(splits[5], (2, C), jnp.float32), 0.25, 1.75)
    tri_qk = gaussian(splits[6], (2, C, 2 * C), (C // 9) ** -0.5, 1.5)
    tri_vg = gaussian(splits[7], (2, C, 2 * C), C ** -0.5, 0.5)
    tri_out = gaussian(splits[8], (2, C, C), C ** -0.5, 0.5)
    bias_gain = jnp.clip(1.0 + 0.15 * jax.random.normal(splits[9], (C,), jnp.float32), 0.25, 1.75)
    bias_proj = gaussian(splits[10], (C, HEADS), C ** -0.5, 0.5)
    chain_bias = gaussian(splits[11], (HEADS,), 1.0, 4.0, ((0, 4),), jnp.float32)
    pos_slope = jnp.clip(jax.random.uniform(splits[12], (HEADS,), jnp.float32, -6.0, 6.0) * levels(splits[12], (HEADS,), ((0, 4),), -0.4, 0.0), -6.0, 6.0)
    attn_gain = jnp.clip(1.0 + 0.15 * jax.random.normal(splits[13], (D,), jnp.float32), 0.25, 1.75)
    attn_qk = gaussian(splits[14], (2, D, D), (D // 3) ** -0.5, 0.375, ((2, 4),))
    attn_vg = gaussian(splits[15], (2, D, D), D ** -0.5, 0.21875, ((2, 4),))
    attn_out = gaussian(splits[16], (D, D), (D // 16) ** -0.5, 0.875, ((0, 4),))
    return {"pair_act": pair_act, "single": single, "token_mask": token_mask, "chain_index": chain_index, "residue_index": residue_index, "tri_gain": tri_gain, "tri_qk": tri_qk, "tri_vg": tri_vg, "tri_out": tri_out, "bias_gain": bias_gain, "bias_proj": bias_proj, "chain_bias": chain_bias, "pos_slope": pos_slope, "attn_gain": attn_gain, "attn_qk": attn_qk, "attn_vg": attn_vg, "attn_out": attn_out}


epsilon = 1e-05
cap_value = 10.0
rel_reach = 32.0
highest = lax.Precision.HIGHEST

def layer_norm(inputs, norm_gain):
    inputs = inputs.astype(jnp.float32)
    centered = inputs - lax.optimization_barrier(jnp.mean(inputs, -1, keepdims=True))
    spread = lax.optimization_barrier(jnp.mean(centered * centered, -1, keepdims=True))
    return centered * lax.rsqrt(spread + epsilon) * norm_gain

def feature(inputs):
    return jnp.where(inputs > 0, inputs + 1.0, jnp.exp(jnp.minimum(inputs, 0.0)))

def rounded(inputs):
    return lax.optimization_barrier(inputs.astype(jnp.bfloat16)).astype(jnp.float32)

def split_heads(inputs):
    return inputs.reshape(inputs.shape[:-1] + (TRI_HEADS, TRI_DIM))

def reference(pair_act, single, token_mask, chain_index, residue_index, tri_gain, tri_qk, tri_vg, tri_out, bias_gain, bias_proj, chain_bias, pos_slope, attn_gain, attn_qk, attn_vg, attn_out):
    block_rows = TOKENS // N_ROW
    mask_float = token_mask.astype(jnp.float32)
    tri_scale = 1.0 / (2.0 * TRI_DIM * math.sqrt(TOKENS))

    def row_pass(row_block):
        normed = layer_norm(row_block, tri_gain[0]).astype(jnp.bfloat16)
        query_key = jnp.dot(normed, tri_qk[0], preferred_element_type=jnp.float32)
        value_gate = jnp.dot(normed, tri_vg[0], preferred_element_type=jnp.float32)
        query_feat = feature(split_heads(query_key[..., :C]))
        key_feat = feature(split_heads(query_key[..., C:])) * mask_float[None, :, None, None]
        values = split_heads(value_gate[..., :C])
        states = jnp.einsum('ijhe,ijhf->ihef', key_feat, values, precision=highest)
        mixed_heads = tri_scale * jnp.einsum('ijhe,ihef->ijhf', query_feat, states, precision=highest)
        gate_part = value_gate[..., C:]
        update = (jax.nn.sigmoid(gate_part) * mixed_heads.reshape(gate_part.shape)).astype(jnp.bfloat16)
        return (row_block.astype(jnp.float32) + jnp.dot(update, tri_out[0], preferred_element_type=jnp.float32)).astype(jnp.bfloat16)
    pair_first = lax.map(row_pass, pair_act.reshape(N_ROW, block_rows, TOKENS, C))
    row_masks = mask_float.reshape(N_ROW, block_rows)

    def col_states(states, inputs):
        row_block, row_mask = inputs
        normed = layer_norm(row_block, tri_gain[1]).astype(jnp.bfloat16)
        key_feat = feature(split_heads(jnp.dot(normed, tri_qk[1][:, C:], preferred_element_type=jnp.float32)))
        key_feat = key_feat * row_mask[:, None, None, None]
        values = split_heads(jnp.dot(normed, tri_vg[1][:, :C], preferred_element_type=jnp.float32))
        return (states + jnp.einsum('ijhe,ijhf->jhef', key_feat, values, precision=highest), None)
    zero_states = jnp.zeros((TOKENS, TRI_HEADS, TRI_DIM, TRI_DIM), jnp.float32)
    states, unused = lax.scan(col_states, zero_states, (pair_first, row_masks))

    def col_pass(row_block):
        normed = layer_norm(row_block, tri_gain[1]).astype(jnp.bfloat16)
        query_feat = feature(split_heads(jnp.dot(normed, tri_qk[1][:, :C], preferred_element_type=jnp.float32)))
        gate_part = jnp.dot(normed, tri_vg[1][:, C:], preferred_element_type=jnp.float32)
        mixed_heads = tri_scale * jnp.einsum('ijhe,jhef->ijhf', query_feat, states, precision=highest)
        update = (jax.nn.sigmoid(gate_part) * mixed_heads.reshape(gate_part.shape)).astype(jnp.bfloat16)
        return (row_block.astype(jnp.float32) + jnp.dot(update, tri_out[1], preferred_element_type=jnp.float32)).astype(jnp.bfloat16)
    pair_second = lax.map(col_pass, pair_first)
    tok_normed = layer_norm(single, attn_gain).astype(jnp.bfloat16)
    query_all = rounded(jnp.dot(tok_normed, attn_qk[0], preferred_element_type=jnp.float32)).reshape(TOKENS, HEADS, HEAD_DIM)
    key_heads = rounded(jnp.dot(tok_normed, attn_qk[1], preferred_element_type=jnp.float32)).reshape(TOKENS, HEADS, HEAD_DIM)
    value_heads = rounded(jnp.dot(tok_normed, attn_vg[0], preferred_element_type=jnp.float32)).reshape(TOKENS, HEADS, HEAD_DIM)
    gate_all = jnp.dot(tok_normed, attn_vg[1], preferred_element_type=jnp.float32)

    def diffuse(inputs):
        pair_rows, query_rows, gate_rows, chain_rows, residue_rows = inputs
        normed = layer_norm(pair_rows, bias_gain).astype(jnp.bfloat16)
        pair_bias = rounded(jnp.dot(normed, bias_proj, preferred_element_type=jnp.float32))
        scores = jnp.einsum('ihd,jhd->hij', query_rows, key_heads, precision=highest) / math.sqrt(HEAD_DIM)
        scores = scores + jnp.transpose(pair_bias, (2, 0, 1))
        same_chain = chain_rows[:, None] == chain_index[None, :]
        offset = jnp.clip((residue_rows[:, None] - residue_index[None, :]).astype(jnp.float32), -rel_reach, rel_reach) / rel_reach
        scores = scores + jnp.where(same_chain[None], chain_bias[:, None, None] + pos_slope[:, None, None] * offset[None], 0.0)
        weights = jnp.exp(cap_value * jnp.tanh(scores / cap_value)) * mask_float[None, None, :]
        numerator = jnp.einsum('hij,jhd->ihd', rounded(weights), value_heads, precision=highest)
        denominator = lax.optimization_barrier(jnp.sum(weights, axis=2))
        attended = numerator / jnp.transpose(denominator)[:, :, None]
        gated = (jax.nn.sigmoid(gate_rows) * attended.reshape(gate_rows.shape)).astype(jnp.bfloat16)
        return jnp.dot(gated, attn_out, preferred_element_type=jnp.float32).astype(jnp.bfloat16)
    token_update = lax.map(diffuse, (pair_second, query_all.reshape(N_ROW, block_rows, HEADS, HEAD_DIM), gate_all.reshape(N_ROW, block_rows, D), chain_index.reshape(N_ROW, block_rows), residue_index.reshape(N_ROW, block_rows)))
    return (pair_second.reshape(TOKENS, TOKENS, C), token_update.reshape(TOKENS, D))
```

```python
import functools
import math

import jax
import jax.numpy as jnp
from jax import lax
from jax.experimental import pallas as pl
from jax.experimental.pallas import tpu as pltpu
from jax.sharding import PartitionSpec as P

C = 128
TRI_HEADS = 8
TRI_DIM = 16
HEAD_DIM = 48

epsilon = 1e-05
cap_value = 10.0
rel_reach = 32.0
MESH = pl.DeviceIdType.MESH
f32 = jnp.float32
bf16 = jnp.bfloat16


def layer_norm(inputs, norm_gain):
    inputs = inputs.astype(f32)
    centered = inputs - jnp.mean(inputs, -1, keepdims=True)
    spread = jnp.mean(centered * centered, -1, keepdims=True)
    return centered * lax.rsqrt(spread + epsilon) * norm_gain


def feature(inputs):
    return jnp.where(inputs > 0, inputs + 1.0, jnp.exp(jnp.minimum(inputs, 0.0)))


def sigmoid(inputs):
    return 1.0 / (1.0 + jnp.exp(-inputs))


def dot(left, right):
    return jnp.dot(left, right, preferred_element_type=f32)


def dot_nt(left, right):
    return lax.dot_general(left, right, (((1,), (1,)), ((), ())), preferred_element_type=f32)


def dot_tn(left, right):
    return lax.dot_general(left, right, (((0,), (0,)), ((), ())), preferred_element_type=f32)


def iota(shape, dim):
    return lax.broadcasted_iota(jnp.int32, shape, dim)


def log2(number):
    power = number.bit_length() - 1
    assert 1 << power == number
    return power


def kernel(
    n_row,
    n_col,
    pair_ref,
    single_ref,
    mask_ref,
    chain_ref,
    residue_ref,
    gain_ref,
    qk_ref,
    vg_ref,
    out_ref,
    bias_gain_ref,
    bias_proj_ref,
    chain_bias_ref,
    slope_ref,
    attn_gain_ref,
    aqk_ref,
    avg_ref,
    aout_ref,
    pair_out_ref,
    token_ref,
    row_part,
    row_recv,
    col_part,
    col_recv,
    col_full,
    q_wide,
    kv,
    bias_acc,
    bias_send,
    bias_recv,
    term_send,
    term_recv,
    row_send_sem,
    row_recv_sem,
    rs_send_sem,
    rs_recv_sem,
    ag_send_sem,
    ag_recv_sem,
    kv_send_sem,
    kv_recv_sem,
    bias_send_sem,
    bias_recv_sem,
    term_send_sem,
    term_recv_sem,
):
    my_row = lax.axis_index("row")
    my_col = lax.axis_index("col")
    rows, cols, _ = pair_ref.shape
    tokens = mask_ref.shape[1]
    flat = rows * cols
    row_first = my_row * rows
    col_first = my_col * cols
    heads_here = chain_bias_ref.shape[1]
    width = token_ref.shape[1]
    tri_scale = 1.0 / (2.0 * TRI_DIM * math.sqrt(tokens))
    col_peers = [lax.rem(my_col + d, n_col) for d in range(n_col)]
    row_peers = [lax.rem(my_row + d, n_row) for d in range(n_row)]

    def push(src, dst, send_sem, recv_sem, where):
        copy = pltpu.make_async_remote_copy(
            src_ref=src, dst_ref=dst, send_sem=send_sem, recv_sem=recv_sem,
            device_id=where, device_id_type=MESH,
        )
        copy.start()
        return copy

    barrier = pltpu.get_barrier_semaphore()
    for d in range(1, n_col):
        pl.semaphore_signal(barrier, inc=1, device_id={"col": col_peers[d]}, device_id_type=MESH)
    for d in range(1, n_row):
        pl.semaphore_signal(barrier, inc=1, device_id={"row": row_peers[d]}, device_id_type=MESH)

    length = jnp.sum(mask_ref[...].astype(f32), axis=1, keepdims=True)

    pair = pair_ref[...].reshape(flat, C)
    normed = layer_norm(pair, gain_ref[0:1, :]).astype(bf16)
    key_value = dot(normed, jnp.concatenate([qk_ref[0, :, C:], vg_ref[0, :, :C]], axis=1))
    col_pos = (iota((1, cols, C), 1) + col_first).astype(f32)
    col_keep = col_pos < length.reshape(1, 1, 1)
    key_feat = jnp.where(col_keep, feature(key_value[:, :C]).reshape(rows, cols, C), 0.0).astype(bf16)
    values = key_value[:, C:].astype(bf16).reshape(rows, cols, C)
    dim_shift = log2(TRI_DIM)
    left = iota((C, C), 0)
    right = iota((C, C), 1)
    same_head = (left >> dim_shift) == (right >> dim_shift)
    for i in range(rows):
        outer = jnp.where(same_head, dot_tn(key_feat[i], values[i]), 0.0)
        row_part[i] = jnp.sum(outer.reshape(TRI_HEADS, TRI_DIM, C), axis=0).astype(bf16)
    pl.semaphore_wait(barrier, n_row + n_col - 2)
    sent = []
    row_copies = []
    for d in range(1, n_col):
        row_copies.append(push(row_part, row_recv.at[d - 1], row_send_sem.at[d - 1],
                               row_recv_sem.at[d - 1], {"col": col_peers[d]}))

    tok = layer_norm(single_ref[...], attn_gain_ref[...]).astype(bf16)
    kv[my_row, 0] = dot(tok, aqk_ref[1]).astype(bf16)
    kv[my_row, 1] = dot(tok, avg_ref[0]).astype(bf16)
    kv_copies = []
    for d in range(1, n_row):
        kv_copies.append(push(kv.at[my_row], kv.at[my_row], kv_send_sem.at[d - 1],
                              kv_recv_sem.at[d - 1], {"row": row_peers[d]}))
    query_gate = dot(normed, jnp.concatenate([qk_ref[0, :, :C], vg_ref[0, :, C:]], axis=1))
    query_feat = feature(query_gate[:, :C]).astype(bf16).reshape(rows, cols, C)
    gate = sigmoid(query_gate[:, C:]) * tri_scale
    tok_query = dot(tok, aqk_ref[0]).astype(bf16)
    tok_gate = sigmoid(dot(tok, avg_ref[1]))

    for copy in row_copies:
        copy.wait_recv()
    states = row_part[...].astype(f32)
    for d in range(1, n_col):
        states = states + row_recv[d - 1].astype(f32)
    states = states.astype(bf16)
    mixed = []
    for i in range(rows):
        block = jnp.concatenate([states[i]] * TRI_HEADS, axis=0)
        block = jnp.where(same_head, block, jnp.zeros_like(block))
        mixed.append(dot(query_feat[i], block))
    mixed = jnp.concatenate(mixed, axis=0)
    update = (gate * mixed).astype(bf16)
    pair = (pair.astype(f32) + dot(update, out_ref[0])).astype(bf16)

    normed = layer_norm(pair, gain_ref[1:2, :]).astype(bf16)
    key_value = dot(normed, jnp.concatenate([qk_ref[1, :, C:], vg_ref[1, :, :C]], axis=1))
    row_pos = (iota((rows, 1, C), 0) + row_first).astype(f32)
    row_keep = row_pos < length.reshape(1, 1, 1)
    key_feat = jnp.where(row_keep, feature(key_value[:, :C]).reshape(rows, cols, C), 0.0)
    key_feat = key_feat.astype(bf16).reshape(flat, C)
    values = key_value[:, C:]
    entry = jnp.where(same_head, left & (TRI_DIM - 1), -1)
    share = TRI_DIM // n_row
    rs_copies = []
    for d in list(range(1, n_row)) + [0]:
        owner = row_peers[d]
        for s in range(share):
            spread = (entry == owner * share + s).astype(f32).astype(bf16)
            wide = dot(key_feat, spread) * values
            col_part[owner, s] = jnp.sum(wide.reshape(rows, cols, C), axis=0).astype(bf16)
        if d:
            rs_copies.append(push(col_part.at[owner], col_recv.at[d - 1], rs_send_sem.at[d - 1],
                                  rs_recv_sem.at[d - 1], {"row": owner}))
    query_gate = dot(normed, jnp.concatenate([qk_ref[1, :, :C], vg_ref[1, :, C:]], axis=1))
    query_feat = feature(query_gate[:, :C]).astype(bf16)
    gate = sigmoid(query_gate[:, C:]) * tri_scale
    for e in range(TRI_DIM):
        spread = (entry == e).astype(f32).astype(bf16)
        q_wide[e] = dot(query_feat, spread).astype(bf16)
    for copy in rs_copies:
        copy.wait_recv()
    total = col_part[my_row].astype(f32)
    for d in range(1, n_row):
        total = total + col_recv[d - 1].astype(f32)
    col_full[my_row] = total.astype(bf16)
    ag_copies = []
    for d in range(1, n_row):
        ag_copies.append(push(col_full.at[my_row], col_full.at[my_row], ag_send_sem.at[d - 1],
                              ag_recv_sem.at[d - 1], {"row": row_peers[d]}))

    for copy in kv_copies:
        copy.wait_recv()
    head_shift = log2(heads_here)
    lines = rows * heads_here
    keys = kv[:, 0].reshape(tokens, width)
    vals = kv[:, 1].reshape(tokens, width)
    line = iota((lines, rows), 0)
    repeat = ((line >> head_shift) == iota((lines, rows), 1)).astype(f32).astype(bf16)
    line_head = iota((lines, width), 0) & (heads_here - 1)
    lane = iota((lines, width), 1)
    own_lanes = (lane >= line_head * HEAD_DIM) & (lane < (line_head + 1) * HEAD_DIM)
    queries = jnp.where(own_lanes, dot(repeat, tok_query), 0.0).astype(bf16)
    scores = dot_nt(queries, keys) * (1.0 / math.sqrt(HEAD_DIM))
    here = iota((lines, tokens), 1) == (iota((lines, tokens), 0) >> head_shift) + row_first
    chain = chain_ref[...].astype(f32)
    residue = residue_ref[...].astype(f32)
    my_chain = jnp.sum(jnp.where(here, chain, 0.0), axis=1, keepdims=True)
    my_residue = jnp.sum(jnp.where(here, residue, 0.0), axis=1, keepdims=True)
    own_head = iota((lines, heads_here), 1) == (iota((lines, heads_here), 0) & (heads_here - 1))
    my_bias = jnp.sum(jnp.where(own_head, chain_bias_ref[...], 0.0), axis=1, keepdims=True)
    my_slope = jnp.sum(jnp.where(own_head, slope_ref[...], 0.0), axis=1, keepdims=True)
    offset = jnp.clip(my_residue - residue, -rel_reach, rel_reach) * (1.0 / rel_reach)
    scores = scores + jnp.where(my_chain == chain, my_bias + my_slope * offset, 0.0)

    group = 8 // heads_here
    picks = n_col * 8
    pick = iota((picks, TRI_DIM), 0)
    wanted = (pick >> 3) * heads_here + (pick & (heads_here - 1))
    chosen = (iota((picks, TRI_DIM), 1) == wanted).astype(f32).astype(bf16)
    picked = dot_nt(chosen, bias_proj_ref[...])
    place = (iota((picks, C), 0) & 7) >> head_shift
    picked = jnp.concatenate([jnp.where(place == g, picked, 0.0) for g in range(group)], axis=1)
    picked = picked.astype(bf16)
    put = (iota((cols, tokens), 0) + col_first == iota((cols, tokens), 1)).astype(f32).astype(bf16)

    def mix(chunk):
        part = None
        for s in range(share):
            here = chunk * share + s
            term = (q_wide[here].astype(f32).reshape(rows, cols, C)
                    * col_full[chunk, s].astype(f32).reshape(1, cols, C))
            part = term if part is None else part + term
        return part

    mixed = mix(my_row)
    for d in range(1, n_row):
        ag_copies[d - 1].wait_recv()
        mixed = mixed + mix(lax.rem(my_row + n_row - d, n_row))
    update = (gate * mixed.reshape(flat, C)).astype(bf16)
    pair = (pair.astype(f32) + dot(update, out_ref[1])).astype(bf16)
    pair_out_ref[...] = pair.reshape(rows, cols, C)

    normed = layer_norm(pair, bias_gain_ref[...]).astype(bf16).reshape(rows, cols, C)
    for i in range(0, rows, group):
        both = jnp.concatenate([normed[i + g] for g in range(group)], axis=1)
        piece = dot(dot_nt(picked, both).astype(bf16), put)
        for c in range(n_col):
            bias_acc[c, i * heads_here:(i + group) * heads_here] = piece[c * 8:(c + 1) * 8]
    bias_send[...] = bias_acc[...].astype(bf16)
    bias_copies = []
    for d in range(1, n_col):
        bias_copies.append(push(bias_send.at[col_peers[d]], bias_recv.at[d - 1], bias_send_sem.at[d - 1],
                                bias_recv_sem.at[d - 1], {"col": col_peers[d]}))
    scores = scores + bias_send[my_col].astype(f32)
    for d in range(1, n_col):
        bias_copies[d - 1].wait_recv()
        scores = scores + bias_recv[d - 1].astype(f32)

    real = iota((lines, tokens), 1).astype(f32) < length
    weights = jnp.where(real, jnp.exp(cap_value * jnp.tanh(scores * (1.0 / cap_value))), 0.0)
    bottom = jnp.sum(weights, axis=1, keepdims=True)
    attended = dot(weights.astype(bf16), vals) / bottom
    attended = jnp.where(own_lanes, attended, 0.0)
    attended = jnp.sum(attended.reshape(rows, heads_here, width), axis=1)
    gated = (tok_gate * attended).astype(bf16)
    terms = dot(gated, aout_ref[...])
    for c in range(n_col):
        term_send[c] = terms[:, c * width:(c + 1) * width].astype(bf16)
    term_copies = []
    for d in range(1, n_col):
        term_copies.append(push(term_send.at[col_peers[d]], term_recv.at[d - 1], term_send_sem.at[d - 1],
                                term_recv_sem.at[d - 1], {"col": col_peers[d]}))
    total = term_send[my_col].astype(f32)
    for d in range(1, n_col):
        term_copies[d - 1].wait_recv()
        total = total + term_recv[d - 1].astype(f32)
    token_ref[...] = total.astype(bf16)
    for copy in row_copies + kv_copies + rs_copies + ag_copies + bias_copies + term_copies:
        copy.wait_send()


def on_device(n_row, n_col, pair_act, single, token_mask, chain_index, residue_index, tri_gain, tri_qk,
              tri_vg, tri_out, bias_gain, bias_proj, chain_bias, pos_slope, attn_gain, attn_qk, attn_vg,
              attn_out):
    rows, cols, _ = pair_act.shape
    tokens = token_mask.shape[0]
    width = attn_qk.shape[2]
    lines = rows * chain_bias.shape[0]
    share = TRI_DIM // n_row
    sems = lambda count: [pltpu.SemaphoreType.DMA((count,))] * 2
    vmem = pl.BlockSpec(memory_space=pltpu.VMEM)
    return pl.pallas_call(
        functools.partial(kernel, n_row, n_col),
        out_shape=(
            jax.ShapeDtypeStruct(pair_act.shape, bf16),
            jax.ShapeDtypeStruct((rows, width), bf16),
        ),
        in_specs=[vmem] * 17,
        out_specs=(vmem, vmem),
        scratch_shapes=[
            pltpu.VMEM((rows, TRI_DIM, C), bf16),
            pltpu.VMEM((n_col - 1, rows, TRI_DIM, C), bf16),
            pltpu.VMEM((n_row, share, cols, C), bf16),
            pltpu.VMEM((n_row - 1, share, cols, C), bf16),
            pltpu.VMEM((n_row, share, cols, C), bf16),
            pltpu.VMEM((TRI_DIM, rows * cols, C), bf16),
            pltpu.VMEM((n_row, 2, rows, width), bf16),
            pltpu.VMEM((n_col, lines, tokens), f32),
            pltpu.VMEM((n_col, lines, tokens), bf16),
            pltpu.VMEM((n_col - 1, lines, tokens), bf16),
            pltpu.VMEM((n_col, rows, width), bf16),
            pltpu.VMEM((n_col - 1, rows, width), bf16),
        ] + sems(n_col - 1) + sems(n_row - 1) + sems(n_row - 1) + sems(n_row - 1) + sems(n_col - 1)
        + sems(n_col - 1),
        compiler_params=pltpu.CompilerParams(
            collective_id=0, has_side_effects=True, vmem_limit_bytes=50 * 1024 * 1024
        ),
    )(
        pair_act, single, token_mask.reshape(1, -1), chain_index.reshape(1, -1),
        residue_index.reshape(1, -1), tri_gain, tri_qk, tri_vg, tri_out, bias_gain.reshape(1, -1),
        bias_proj, chain_bias.reshape(1, -1), pos_slope.reshape(1, -1), attn_gain.reshape(1, -1),
        attn_qk, attn_vg, attn_out,
    )


def solution(mesh):
    return jax.shard_map(
        functools.partial(on_device, mesh.shape["row"], mesh.shape["col"]),
        mesh=mesh,
        in_specs=(
            P(("grp", "row"), "col", None),
            P(("grp", "row"), None),
            P("grp"),
            P("grp"),
            P("grp"),
            P(),
            P(),
            P(),
            P(),
            P(),
            P(),
            P("col"),
            P("col"),
            P(),
            P(None, None, "col"),
            P(None, None, "col"),
            P("col", None),
        ),
        out_specs=(P(("grp", "row"), "col", None), P(("grp", "row"), "col")),
        check_vma=False,
    )
```

```python
import functools
import math

import jax
import jax.numpy as jnp
from jax import lax
from jax.experimental import pallas as pl
from jax.experimental.pallas import tpu as pltpu
from jax.sharding import PartitionSpec as P

C = 128
TRI_HEADS = 8
TRI_DIM = 16
HEAD_DIM = 48

epsilon = 1e-05
cap_value = 10.0
rel_reach = 32.0
MESH = pl.DeviceIdType.MESH
f32 = jnp.float32
bf16 = jnp.bfloat16


def layer_norm(inputs, norm_gain):
    inputs = inputs.astype(f32)
    centered = inputs - jnp.mean(inputs, -1, keepdims=True)
    spread = jnp.mean(centered * centered, -1, keepdims=True)
    return centered * lax.rsqrt(spread + epsilon) * norm_gain


def feature(inputs):
    return jnp.where(inputs > 0, inputs + 1.0, jnp.exp(jnp.minimum(inputs, 0.0)))


def sigmoid(inputs):
    return 1.0 / (1.0 + jnp.exp(-inputs))


def dot(left, right):
    return jnp.dot(left, right, preferred_element_type=f32)


def dot_nt(left, right):
    return lax.dot_general(left, right, (((1,), (1,)), ((), ())), preferred_element_type=f32)


def dot_tn(left, right):
    return lax.dot_general(left, right, (((0,), (0,)), ((), ())), preferred_element_type=f32)


def iota(shape, dim):
    return lax.broadcasted_iota(jnp.int32, shape, dim)


def log2(number):
    power = number.bit_length() - 1
    assert 1 << power == number
    return power


def kernel(
    n_row,
    n_col,
    pair_ref,
    single_ref,
    mask_ref,
    chain_ref,
    residue_ref,
    gain_ref,
    qk_ref,
    vg_ref,
    out_ref,
    bias_gain_ref,
    bias_proj_ref,
    chain_bias_ref,
    slope_ref,
    attn_gain_ref,
    aqk_hbm,
    avg_hbm,
    aout_hbm,
    pair_out_ref,
    token_ref,
    aqk_ref,
    avg_ref,
    aout_ref,
    row_part,
    row_recv,
    col_part,
    col_recv,
    col_full,
    q_wide,
    kv,
    kv_own,
    query_gates,
    rel,
    aout_send,
    aout_full,
    num_send,
    num_recv,
    den_send,
    den_recv,
    load_sem,
    row_send_sem,
    row_recv_sem,
    rs_send_sem,
    rs_recv_sem,
    ag_send_sem,
    ag_recv_sem,
    kv_send_sem,
    kv_recv_sem,
    own_send_sem,
    own_recv_sem,
    qg_send_sem,
    qg_recv_sem,
    rel_send_sem,
    rel_recv_sem,
    aout_send_sem,
    aout_recv_sem,
    num_send_sem,
    num_recv_sem,
    den_send_sem,
    den_recv_sem,
):
    my_row = lax.axis_index("row")
    my_col = lax.axis_index("col")
    rows, cols, _ = pair_ref.shape
    tokens = mask_ref.shape[1]
    flat = rows * cols
    row_first = my_row * rows
    col_first = my_col * cols
    heads_here = chain_bias_ref.shape[1]
    heads = heads_here * n_col
    width = token_ref.shape[1]
    per = cols // rows
    tri_scale = 1.0 / (2.0 * TRI_DIM * math.sqrt(tokens))
    col_peers = [lax.rem(my_col + d, n_col) for d in range(n_col)]
    row_peers = [lax.rem(my_row + d, n_row) for d in range(n_row)]
    far_first = sorted(range(1, n_row), key=lambda d: abs(2 * d - n_row))
    pushed = []

    def push(src, dst, send_sem, recv_sem, where):
        copy = pltpu.make_async_remote_copy(
            src_ref=src, dst_ref=dst, send_sem=send_sem, recv_sem=recv_sem,
            device_id=where, device_id_type=MESH,
        )
        copy.start()
        pushed.append(copy)
        return copy

    def push_cols(src_of, dst_of, send_sem, recv_sem):
        return [
            push(src_of(d), dst_of(d), send_sem.at[d - 1], recv_sem.at[d - 1], {"col": col_peers[d]})
            for d in range(1, n_col)
        ]

    barrier = pltpu.get_barrier_semaphore()
    for d in range(1, n_col):
        pl.semaphore_signal(barrier, inc=1, device_id={"col": col_peers[d]}, device_id_type=MESH)
    for d in range(1, n_row):
        pl.semaphore_signal(barrier, inc=1, device_id={"row": row_peers[d]}, device_id_type=MESH)
    loads = []
    for position, (src, dst) in enumerate(((aqk_hbm, aqk_ref), (avg_hbm, avg_ref), (aout_hbm, aout_ref))):
        loads.append(pltpu.make_async_copy(src, dst, load_sem.at[position]))
        loads[-1].start()

    length = jnp.sum(mask_ref[...].astype(f32), axis=1, keepdims=True)

    pair = pair_ref[...].reshape(flat, C)
    normed = layer_norm(pair, gain_ref[0:1, :]).astype(bf16)
    key_value = dot(normed, jnp.concatenate([qk_ref[0, :, C:], vg_ref[0, :, :C]], axis=1))
    col_pos = (iota((1, cols, C), 1) + col_first).astype(f32)
    col_keep = col_pos < length.reshape(1, 1, 1)
    key_feat = jnp.where(col_keep, feature(key_value[:, :C]).reshape(rows, cols, C), 0.0).astype(bf16)
    values = key_value[:, C:].astype(bf16).reshape(rows, cols, C)
    dim_shift = log2(TRI_DIM)
    left = iota((C, C), 0)
    right = iota((C, C), 1)
    same_head = (left >> dim_shift) == (right >> dim_shift)
    for i in range(rows):
        outer = jnp.where(same_head, dot_tn(key_feat[i], values[i]), 0.0)
        row_part[i] = jnp.sum(outer.reshape(TRI_HEADS, TRI_DIM, C), axis=0).astype(bf16)
    pl.semaphore_wait(barrier, n_row + n_col - 2)
    row_copies = push_cols(lambda d: row_part, lambda d: row_recv.at[d - 1], row_send_sem, row_recv_sem)

    lane = iota((8, C), 1)
    top = iota((8, C), 0) == 0
    relation = jnp.zeros((8, C), f32)
    for h in range(heads_here):
        pick = jnp.where(top, chain_bias_ref[:, h:h + 1], slope_ref[:, h:h + 1])
        relation = relation + jnp.where(lane == my_col * heads_here + h, pick, 0.0)
    rel[my_col] = relation
    rel_copies = push_cols(lambda d: rel.at[my_col], lambda d: rel.at[my_col], rel_send_sem, rel_recv_sem)
    tok = layer_norm(single_ref[...], attn_gain_ref[...]).astype(bf16)
    loads[0].wait()
    loads[1].wait()
    kv[my_row, 0] = dot_nt(tok, aqk_ref[1]).astype(bf16)
    kv[my_row, 1] = dot_nt(tok, avg_ref[0]).astype(bf16)
    kv_copies = {}
    for d in far_first:
        kv_copies[d] = push(kv.at[my_row], kv.at[my_row], kv_send_sem.at[d - 1],
                            kv_recv_sem.at[d - 1], {"row": row_peers[d]})
    query_gate = dot(normed, jnp.concatenate([qk_ref[0, :, :C], vg_ref[0, :, C:]], axis=1))
    query_feat = feature(query_gate[:, :C]).astype(bf16).reshape(rows, cols, C)
    gate = sigmoid(query_gate[:, C:]) * tri_scale
    query_gates[my_col, 0] = dot_nt(tok, aqk_ref[0]).astype(bf16)
    query_gates[my_col, 1] = sigmoid(dot_nt(tok, avg_ref[1])).astype(bf16)
    loads[2].wait()
    for c in range(n_col):
        aout_send[c] = aout_ref[:, c * width:(c + 1) * width]
    aout_full[my_col] = aout_send[my_col]

    for copy in row_copies:
        copy.wait_recv()
    qg_copies = push_cols(lambda d: query_gates.at[my_col], lambda d: query_gates.at[my_col],
                          qg_send_sem, qg_recv_sem)
    states = row_part[...].astype(f32)
    for d in range(1, n_col):
        states = states + row_recv[d - 1].astype(f32)
    states = states.astype(bf16)
    mixed = []
    for i in range(rows):
        block = jnp.concatenate([states[i]] * TRI_HEADS, axis=0)
        block = jnp.where(same_head, block, jnp.zeros_like(block))
        mixed.append(dot(query_feat[i], block))
    mixed = jnp.concatenate(mixed, axis=0)
    update = (gate * mixed).astype(bf16)
    pair = (pair.astype(f32) + dot(update, out_ref[0])).astype(bf16)

    normed = layer_norm(pair, gain_ref[1:2, :]).astype(bf16)
    key_value = dot(normed, jnp.concatenate([qk_ref[1, :, C:], vg_ref[1, :, :C]], axis=1))
    row_pos = (iota((rows, 1, C), 0) + row_first).astype(f32)
    row_keep = row_pos < length.reshape(1, 1, 1)
    key_feat = jnp.where(row_keep, feature(key_value[:, :C]).reshape(rows, cols, C), 0.0)
    key_feat = key_feat.astype(bf16).reshape(flat, C)
    values = key_value[:, C:]
    entry = jnp.where(same_head, left & (TRI_DIM - 1), -1)
    share = TRI_DIM // n_row

    def spread(first, count):
        parts = [(entry == first + s).astype(f32).astype(bf16) for s in range(count)]
        return parts[0] if count == 1 else jnp.concatenate(parts, axis=1)

    rs_copies = {}
    for d in far_first + [0]:
        owner = row_peers[d]
        wide = dot(key_feat, spread(owner * share, share))
        for s in range(share):
            part = wide[:, s * C:(s + 1) * C] * values
            col_part[owner, s] = jnp.sum(part.reshape(rows, cols, C), axis=0).astype(bf16)
        if d:
            rs_copies[d] = push(col_part.at[owner], col_recv.at[d - 1], rs_send_sem.at[d - 1],
                                rs_recv_sem.at[d - 1], {"row": owner})
    aout_copies = push_cols(lambda d: aout_send.at[col_peers[d]], lambda d: aout_full.at[my_col],
                            aout_send_sem, aout_recv_sem)
    query_gate = dot(normed, jnp.concatenate([qk_ref[1, :, :C], vg_ref[1, :, C:]], axis=1))
    query_feat = feature(query_gate[:, :C]).astype(bf16)
    gate = sigmoid(query_gate[:, C:]) * tri_scale
    for e in range(0, TRI_DIM, 2):
        wide = dot(query_feat, spread(e, 2)).astype(bf16)
        q_wide[e] = wide[:, :C]
        q_wide[e + 1] = wide[:, C:]
    for d in far_first:
        kv_copies[d].wait_recv()
    kv_own[my_col] = kv[pl.ds(my_col * per, per)]
    own_copies = push_cols(lambda d: kv.at[pl.ds(col_peers[d] * per, per)], lambda d: kv_own.at[my_col],
                           own_send_sem, own_recv_sem)
    total = col_part[my_row].astype(f32)
    for d in far_first:
        rs_copies[d].wait_recv()
        total = total + col_recv[d - 1].astype(f32)
    col_full[my_row] = total.astype(bf16)
    ag_copies = {}
    for d in far_first:
        ag_copies[d] = push(col_full.at[my_row], col_full.at[my_row], ag_send_sem.at[d - 1],
                            ag_recv_sem.at[d - 1], {"row": row_peers[d]})

    head_shift = log2(heads)
    lines = rows * heads
    for copy in rel_copies + qg_copies + own_copies:
        copy.wait_recv()
    head_of = iota((heads, width), 0)
    head_lane = iota((heads, width), 1)
    lanes_of = []
    for c in range(n_col):
        start = (head_of - c * heads_here) * HEAD_DIM
        lanes_of.append((head_lane >= start) & (head_lane < start + HEAD_DIM))
    scores = jnp.zeros((lines, cols), f32)
    for c in range(n_col):
        query = query_gates[c, 0].astype(f32)
        stack = jnp.where(lanes_of[c][None], query[:, None, :], 0.0).reshape(lines, width).astype(bf16)
        scores = scores + dot_nt(stack, kv_own[c, :, 0].reshape(cols, width))
    scores = scores * (1.0 / math.sqrt(HEAD_DIM))
    here = iota((lines, tokens), 1) == (iota((lines, tokens), 0) >> head_shift) + row_first
    chain = chain_ref[...].astype(f32)
    residue = residue_ref[...]
    my_chain = jnp.sum(jnp.where(here, chain, 0.0), axis=1, keepdims=True)
    my_residue = jnp.sum(jnp.where(here, residue.astype(f32), 0.0), axis=1, keepdims=True)
    relation = rel[0]
    for c in range(1, n_col):
        relation = relation + rel[c]
    own_head = iota((lines, C), 1) == (iota((lines, C), 0) & (heads - 1))
    my_bias = jnp.sum(jnp.where(own_head, relation[0:1], 0.0), axis=1, keepdims=True)
    my_slope = jnp.sum(jnp.where(own_head, relation[1:2], 0.0), axis=1, keepdims=True)
    kind = iota((8, tokens), 0)
    facts = jnp.where(kind == 0, chain, jnp.where(kind == 1, (residue >> 4).astype(f32),
                                                  (residue & 15).astype(f32))).astype(bf16)
    take = (iota((tokens, cols), 0) == iota((tokens, cols), 1) + col_first).astype(f32).astype(bf16)
    facts = dot(facts, take)
    offset = my_residue - (facts[1:2] * 16.0 + facts[2:3])
    offset = jnp.clip(offset, -rel_reach, rel_reach) * (1.0 / rel_reach)
    scores = scores + jnp.where(my_chain == facts[0:1], my_bias + my_slope * offset, 0.0)
    real = (iota((lines, cols), 1) + col_first).astype(f32) < length

    def mix(chunk):
        part = None
        for s in range(share):
            term = (q_wide[chunk * share + s].astype(f32).reshape(rows, cols, C)
                    * col_full[chunk, s].astype(f32).reshape(1, cols, C))
            part = term if part is None else part + term
        return part

    mixed = mix(my_row)
    for d in far_first:
        ag_copies[d].wait_recv()
        mixed = mixed + mix(lax.rem(my_row + n_row - d, n_row))
    update = (gate * mixed.reshape(flat, C)).astype(bf16)
    pair = (pair.astype(f32) + dot(update, out_ref[1])).astype(bf16)
    pair_out_ref[...] = pair.reshape(rows, cols, C)

    normed = layer_norm(pair, bias_gain_ref[...]).astype(bf16).reshape(rows, cols, C)
    bias = [dot_nt(bias_proj_ref[...], normed[i]) for i in range(rows)]
    scores = scores + jnp.concatenate(bias, axis=0).astype(bf16).astype(f32)
    weights = jnp.where(real, jnp.exp(cap_value * jnp.tanh(scores * (1.0 / cap_value))), 0.0)
    bottom = jnp.sum(weights, axis=1, keepdims=True)
    weights = weights.astype(bf16)
    diagonal = iota((heads, C), 0) == iota((heads, C), 1)
    bottom = jnp.sum(jnp.where(diagonal[None], bottom.reshape(rows, heads, 1), 0.0), axis=1)
    bottom_high = bottom.astype(bf16)
    den_send[:, :C] = bottom_high
    den_send[:, C:] = (bottom - bottom_high.astype(f32)).astype(bf16)
    tops = []
    for c in range(n_col):
        attended = dot(weights, kv_own[c, :, 1].reshape(cols, width)).reshape(rows, heads, width)
        tops.append(jnp.sum(jnp.where(lanes_of[c][None], attended, 0.0), axis=1))
        num_send[c] = tops[c].astype(bf16)
    den_copies = push_cols(lambda d: den_send, lambda d: den_recv.at[d - 1], den_send_sem, den_recv_sem)
    num_copies = push_cols(lambda d: num_send, lambda d: num_recv.at[d - 1], num_send_sem, num_recv_sem)
    for copy in aout_copies:
        copy.wait_recv()
    deep = iota((2 * C, width), 0) & (C - 1)
    flat_lane = iota((2 * C, width), 1)
    wide_of = []
    for c in range(n_col):
        start = (deep - c * heads_here) * HEAD_DIM
        wide_of.append(((flat_lane >= start) & (flat_lane < start + HEAD_DIM)).astype(f32).astype(bf16))
    for d in range(1, n_col):
        den_copies[d - 1].wait_recv()
        bottom = bottom + (den_recv[d - 1, :, :C].astype(f32) + den_recv[d - 1, :, C:].astype(f32))
    inverse = jnp.where(iota((rows, C), 1) < heads, 1.0 / bottom, 0.0)
    inverse_high = inverse.astype(bf16)
    inverse = jnp.concatenate([inverse_high, (inverse - inverse_high.astype(f32)).astype(bf16)], axis=1)
    factors = [query_gates[c, 1].astype(f32) * dot(inverse, wide_of[c]) for c in range(n_col)]
    for copy in num_copies:
        copy.wait_recv()
    result = jnp.zeros((rows, width), f32)
    for c in range(n_col):
        top = tops[c]
        for d in range(1, n_col):
            top = top + num_recv[d - 1, c].astype(f32)
        result = result + dot((factors[c] * top).astype(bf16), aout_full[c])
    token_ref[...] = result.astype(bf16)
    for copy in pushed:
        copy.wait_send()


def on_device(n_row, n_col, pair_act, single, token_mask, chain_index, residue_index, tri_gain, tri_qk,
              tri_vg, tri_out, bias_gain, bias_proj, chain_bias, pos_slope, attn_gain, attn_qk, attn_vg,
              attn_out):
    rows, cols, _ = pair_act.shape
    width = attn_qk.shape[2]
    share = TRI_DIM // n_row
    per = cols // rows
    by_col = [pltpu.SemaphoreType.DMA((n_col - 1,))] * 2
    by_row = [pltpu.SemaphoreType.DMA((n_row - 1,))] * 2
    vmem = pl.BlockSpec(memory_space=pltpu.VMEM)
    anywhere = pl.BlockSpec(memory_space=pl.ANY)
    return pl.pallas_call(
        functools.partial(kernel, n_row, n_col),
        out_shape=(
            jax.ShapeDtypeStruct(pair_act.shape, bf16),
            jax.ShapeDtypeStruct((rows, width), bf16),
        ),
        in_specs=[vmem] * 14 + [anywhere] * 3,
        out_specs=(vmem, vmem),
        scratch_shapes=[
            pltpu.VMEM((2, width) + attn_qk.shape[1:2], bf16),
            pltpu.VMEM((2, width) + attn_vg.shape[1:2], bf16),
            pltpu.VMEM(attn_out.shape, bf16),
            pltpu.VMEM((rows, TRI_DIM, C), bf16),
            pltpu.VMEM((n_col - 1, rows, TRI_DIM, C), bf16),
            pltpu.VMEM((n_row, share, cols, C), bf16),
            pltpu.VMEM((n_row - 1, share, cols, C), bf16),
            pltpu.VMEM((n_row, share, cols, C), bf16),
            pltpu.VMEM((TRI_DIM, rows * cols, C), bf16),
            pltpu.VMEM((n_row, 2, rows, width), bf16),
            pltpu.VMEM((n_col, per, 2, rows, width), bf16),
            pltpu.VMEM((n_col, 2, rows, width), bf16),
            pltpu.VMEM((n_col, 8, C), f32),
            pltpu.VMEM((n_col, width, width), bf16),
            pltpu.VMEM((n_col, width, width), bf16),
            pltpu.VMEM((n_col, rows, width), bf16),
            pltpu.VMEM((n_col - 1, n_col, rows, width), bf16),
            pltpu.VMEM((rows, 2 * C), bf16),
            pltpu.VMEM((n_col - 1, rows, 2 * C), bf16),
            pltpu.SemaphoreType.DMA((3,)),
        ] + by_col + by_row + by_row + by_row + by_col * 6,
        compiler_params=pltpu.CompilerParams(
            collective_id=0, has_side_effects=True, vmem_limit_bytes=50 * 1024 * 1024
        ),
    )(
        pair_act, single, token_mask.reshape(1, -1), chain_index.reshape(1, -1),
        residue_index.reshape(1, -1), tri_gain, tri_qk, tri_vg, tri_out, bias_gain.reshape(1, -1),
        bias_proj.T, chain_bias.reshape(1, -1), pos_slope.reshape(1, -1), attn_gain.reshape(1, -1),
        jnp.swapaxes(attn_qk, 1, 2), jnp.swapaxes(attn_vg, 1, 2), attn_out,
    )


def solution(mesh):
    return jax.shard_map(
        functools.partial(on_device, mesh.shape["row"], mesh.shape["col"]),
        mesh=mesh,
        in_specs=(
            P(("grp", "row"), "col", None),
            P(("grp", "row"), None),
            P("grp"),
            P("grp"),
            P("grp"),
            P(),
            P(),
            P(),
            P(),
            P(),
            P(),
            P("col"),
            P("col"),
            P(),
            P(None, None, "col"),
            P(None, None, "col"),
            P("col", None),
        ),
        out_specs=(P(("grp", "row"), "col", None), P(("grp", "row"), "col")),
        check_vma=False,
    )
```

```python
import functools
import math

import jax
import jax.numpy as jnp
from jax import lax
from jax.experimental import pallas as pl
from jax.experimental.pallas import tpu as pltpu
from jax.sharding import PartitionSpec as P

C = 128
TRI_HEADS = 8
TRI_DIM = 16
HEAD_DIM = 48

epsilon = 1e-05
cap_value = 10.0
rel_reach = 32.0
MESH = pl.DeviceIdType.MESH
f32 = jnp.float32
bf16 = jnp.bfloat16


def layer_norm(inputs, norm_gain):
    inputs = inputs.astype(f32)
    centered = inputs - jnp.mean(inputs, -1, keepdims=True)
    spread = jnp.mean(centered * centered, -1, keepdims=True)
    return centered * lax.rsqrt(spread + epsilon) * norm_gain


def feature(inputs):
    return jnp.where(inputs > 0, inputs + 1.0, jnp.exp(jnp.minimum(inputs, 0.0)))


def sigmoid(inputs):
    return 1.0 / (1.0 + jnp.exp(-inputs))


def dot(left, right):
    return jnp.dot(left, right, preferred_element_type=f32)


def dot_nt(left, right):
    return lax.dot_general(left, right, (((1,), (1,)), ((), ())), preferred_element_type=f32)


def dot_tn(left, right):
    return lax.dot_general(left, right, (((0,), (0,)), ((), ())), preferred_element_type=f32)


def iota(shape, dim):
    return lax.broadcasted_iota(jnp.int32, shape, dim)


def log2(number):
    power = number.bit_length() - 1
    assert 1 << power == number
    return power


def kernel(
    n_row,
    n_col,
    pair_hbm,
    single_hbm,
    mask_hbm,
    chain_hbm,
    residue_hbm,
    gain_hbm,
    qk_hbm,
    vg_hbm,
    out_hbm,
    bias_gain_hbm,
    bias_proj_hbm,
    chain_bias_hbm,
    slope_hbm,
    attn_gain_hbm,
    aqk_hbm,
    avg_hbm,
    aout_hbm,
    pair_out_hbm,
    token_ref,
    pair_out_ref,
    pair_ref,
    single_ref,
    mask_ref,
    chain_ref,
    residue_ref,
    gain_ref,
    qk_ref,
    vg_ref,
    out_ref,
    bias_gain_ref,
    bias_proj_ref,
    chain_bias_ref,
    slope_ref,
    attn_gain_ref,
    aqk_ref,
    avg_ref,
    aout_ref,
    row_part,
    row_recv,
    col_part,
    col_recv,
    col_full,
    q_wide,
    kv,
    kv_own,
    query_gates,
    rel,
    aout_send,
    aout_full,
    num_send,
    num_recv,
    den_send,
    den_recv,
    load_sem,
    store_sem,
    row_send_sem,
    row_recv_sem,
    rs_send_sem,
    rs_recv_sem,
    ag_send_sem,
    ag_recv_sem,
    kv_send_sem,
    kv_recv_sem,
    own_send_sem,
    own_recv_sem,
    qg_send_sem,
    qg_recv_sem,
    rel_send_sem,
    rel_recv_sem,
    aout_send_sem,
    aout_recv_sem,
    num_send_sem,
    num_recv_sem,
    den_send_sem,
    den_recv_sem,
):
    my_row = lax.axis_index("row")
    my_col = lax.axis_index("col")
    rows, cols, _ = pair_ref.shape
    tokens = mask_ref.shape[1]
    flat = rows * cols
    row_first = my_row * rows
    col_first = my_col * cols
    heads_here = chain_bias_ref.shape[1]
    heads = heads_here * n_col
    width = token_ref.shape[1]
    per = cols // rows
    tri_scale = 1.0 / (2.0 * TRI_DIM * math.sqrt(tokens))
    col_peers = [lax.rem(my_col + d, n_col) for d in range(n_col)]
    row_peers = [lax.rem(my_row + d, n_row) for d in range(n_row)]
    far_first = sorted(range(1, n_row), key=lambda d: abs(2 * d - n_row))
    pushed = []

    def push(src, dst, send_sem, recv_sem, where):
        copy = pltpu.make_async_remote_copy(
            src_ref=src, dst_ref=dst, send_sem=send_sem, recv_sem=recv_sem,
            device_id=where, device_id_type=MESH,
        )
        copy.start()
        pushed.append(copy)
        return copy

    def push_cols(src_of, dst_of, send_sem, recv_sem):
        return [
            push(src_of(d), dst_of(d), send_sem.at[d - 1], recv_sem.at[d - 1], {"col": col_peers[d]})
            for d in range(1, n_col)
        ]

    barrier = pltpu.get_barrier_semaphore()
    for d in range(1, n_col):
        pl.semaphore_signal(barrier, inc=1, device_id={"col": col_peers[d]}, device_id_type=MESH)
    for d in range(1, n_row):
        pl.semaphore_signal(barrier, inc=1, device_id={"row": row_peers[d]}, device_id_type=MESH)
    loads = {}
    for position, (src, dst) in enumerate((
        (pair_hbm, pair_ref), (gain_hbm, gain_ref), (qk_hbm, qk_ref), (vg_hbm, vg_ref), (mask_hbm, mask_ref),
        (single_hbm, single_ref), (attn_gain_hbm, attn_gain_ref), (chain_bias_hbm, chain_bias_ref),
        (slope_hbm, slope_ref), (aqk_hbm, aqk_ref), (avg_hbm, avg_ref), (out_hbm, out_ref), (aout_hbm, aout_ref),
        (chain_hbm, chain_ref), (residue_hbm, residue_ref), (bias_gain_hbm, bias_gain_ref),
        (bias_proj_hbm, bias_proj_ref),
    )):
        loads[id(dst)] = pltpu.make_async_copy(src, dst, load_sem.at[position])
        loads[id(dst)].start()

    def loaded(*refs):
        for ref in refs:
            loads[id(ref)].wait()

    loaded(pair_ref, gain_ref, qk_ref, vg_ref, mask_ref)
    length = jnp.sum(mask_ref[...].astype(f32), axis=1, keepdims=True)

    pair = pair_ref[...].reshape(flat, C)
    normed = layer_norm(pair, gain_ref[0:1, :]).astype(bf16)
    key_value = dot(normed, jnp.concatenate([qk_ref[0, :, C:], vg_ref[0, :, :C]], axis=1))
    col_pos = (iota((1, cols, C), 1) + col_first).astype(f32)
    col_keep = col_pos < length.reshape(1, 1, 1)
    key_feat = jnp.where(col_keep, feature(key_value[:, :C]).reshape(rows, cols, C), 0.0).astype(bf16)
    values = key_value[:, C:].astype(bf16).reshape(rows, cols, C)
    dim_shift = log2(TRI_DIM)
    left = iota((C, C), 0)
    right = iota((C, C), 1)
    same_head = (left >> dim_shift) == (right >> dim_shift)
    for i in range(rows):
        outer = jnp.where(same_head, dot_tn(key_feat[i], values[i]), 0.0)
        row_part[i] = jnp.sum(outer.reshape(TRI_HEADS, TRI_DIM, C), axis=0).astype(bf16)
    pl.semaphore_wait(barrier, n_row + n_col - 2)
    row_copies = push_cols(lambda d: row_part, lambda d: row_recv.at[d - 1], row_send_sem, row_recv_sem)

    loaded(single_ref, attn_gain_ref, chain_bias_ref, slope_ref)
    lane = iota((8, C), 1)
    top = iota((8, C), 0) == 0
    relation = jnp.zeros((8, C), f32)
    for h in range(heads_here):
        pick = jnp.where(top, chain_bias_ref[:, h:h + 1], slope_ref[:, h:h + 1])
        relation = relation + jnp.where(lane == my_col * heads_here + h, pick, 0.0)
    rel[my_col] = relation
    rel_copies = push_cols(lambda d: rel.at[my_col], lambda d: rel.at[my_col], rel_send_sem, rel_recv_sem)
    gains = [attn_gain_ref[g:g + 1, :] for g in range(attn_gain_ref.shape[0])]
    tok = layer_norm(single_ref[...], jnp.concatenate(gains, axis=1)).astype(bf16)
    loaded(aqk_ref, avg_ref)
    kv[my_row, 0] = dot_nt(tok, aqk_ref[1]).astype(bf16)
    kv[my_row, 1] = dot_nt(tok, avg_ref[0]).astype(bf16)
    kv_copies = {}
    for d in far_first:
        kv_copies[d] = push(kv.at[my_row], kv.at[my_row], kv_send_sem.at[d - 1],
                            kv_recv_sem.at[d - 1], {"row": row_peers[d]})
    query_gate = dot(normed, jnp.concatenate([qk_ref[0, :, :C], vg_ref[0, :, C:]], axis=1))
    query_feat = feature(query_gate[:, :C]).astype(bf16).reshape(rows, cols, C)
    gate = sigmoid(query_gate[:, C:]) * tri_scale
    query_gates[my_col, 0] = dot_nt(tok, aqk_ref[0]).astype(bf16)
    query_gates[my_col, 1] = sigmoid(dot_nt(tok, avg_ref[1])).astype(bf16)
    loaded(aout_ref)
    for c in range(n_col):
        aout_send[c] = aout_ref[:, c * width:(c + 1) * width]
    aout_full[my_col] = aout_send[my_col]

    loaded(out_ref, chain_ref, residue_ref, bias_gain_ref, bias_proj_ref)
    for copy in row_copies:
        copy.wait_recv()
    qg_copies = push_cols(lambda d: query_gates.at[my_col], lambda d: query_gates.at[my_col],
                          qg_send_sem, qg_recv_sem)
    states = row_part[...].astype(f32)
    for d in range(1, n_col):
        states = states + row_recv[d - 1].astype(f32)
    states = states.astype(bf16)
    mixed = []
    for i in range(rows):
        block = jnp.concatenate([states[i]] * TRI_HEADS, axis=0)
        block = jnp.where(same_head, block, jnp.zeros_like(block))
        mixed.append(dot(query_feat[i], block))
    mixed = jnp.concatenate(mixed, axis=0)
    update = (gate * mixed).astype(bf16)
    pair = (pair.astype(f32) + dot(update, out_ref[0])).astype(bf16)

    normed = layer_norm(pair, gain_ref[1:2, :]).astype(bf16)
    key_value = dot(normed, jnp.concatenate([qk_ref[1, :, C:], vg_ref[1, :, :C]], axis=1))
    row_pos = (iota((rows, 1, C), 0) + row_first).astype(f32)
    row_keep = row_pos < length.reshape(1, 1, 1)
    key_feat = jnp.where(row_keep, feature(key_value[:, :C]).reshape(rows, cols, C), 0.0)
    key_feat = key_feat.astype(bf16).reshape(flat, C)
    values = key_value[:, C:]
    entry = jnp.where(same_head, left & (TRI_DIM - 1), -1)
    share = TRI_DIM // n_row

    def spread(first, count):
        parts = [(entry == first + s).astype(f32).astype(bf16) for s in range(count)]
        return parts[0] if count == 1 else jnp.concatenate(parts, axis=1)

    rs_copies = {}
    for d in far_first + [0]:
        owner = row_peers[d]
        wide = dot(key_feat, spread(owner * share, share))
        for s in range(share):
            part = wide[:, s * C:(s + 1) * C] * values
            col_part[owner, s] = jnp.sum(part.reshape(rows, cols, C), axis=0).astype(bf16)
        if d:
            rs_copies[d] = push(col_part.at[owner], col_recv.at[d - 1], rs_send_sem.at[d - 1],
                                rs_recv_sem.at[d - 1], {"row": owner})
    aout_copies = push_cols(lambda d: aout_send.at[col_peers[d]], lambda d: aout_full.at[my_col],
                            aout_send_sem, aout_recv_sem)
    query_gate = dot(normed, jnp.concatenate([qk_ref[1, :, :C], vg_ref[1, :, C:]], axis=1))
    query_feat = feature(query_gate[:, :C]).astype(bf16)
    gate = sigmoid(query_gate[:, C:]) * tri_scale
    for e in range(0, TRI_DIM, 2):
        wide = dot(query_feat, spread(e, 2)).astype(bf16)
        q_wide[e] = wide[:, :C]
        q_wide[e + 1] = wide[:, C:]
    for d in far_first:
        kv_copies[d].wait_recv()
    kv_own[my_col] = kv[pl.ds(my_col * per, per)]
    own_copies = push_cols(lambda d: kv.at[pl.ds(col_peers[d] * per, per)], lambda d: kv_own.at[my_col],
                           own_send_sem, own_recv_sem)
    total = col_part[my_row].astype(f32)
    for d in far_first:
        rs_copies[d].wait_recv()
        total = total + col_recv[d - 1].astype(f32)
    col_full[my_row] = total.astype(bf16)
    ag_copies = {}
    for d in far_first:
        ag_copies[d] = push(col_full.at[my_row], col_full.at[my_row], ag_send_sem.at[d - 1],
                            ag_recv_sem.at[d - 1], {"row": row_peers[d]})

    head_shift = log2(heads)
    lines = rows * heads
    for copy in rel_copies + qg_copies + own_copies:
        copy.wait_recv()
    head_of = iota((heads, width), 0)
    head_lane = iota((heads, width), 1)
    lanes_of = []
    for c in range(n_col):
        start = (head_of - c * heads_here) * HEAD_DIM
        lanes_of.append((head_lane >= start) & (head_lane < start + HEAD_DIM))
    scores = jnp.zeros((lines, cols), f32)
    for c in range(n_col):
        query = query_gates[c, 0].astype(f32)
        stack = jnp.where(lanes_of[c][None], query[:, None, :], 0.0).reshape(lines, width).astype(bf16)
        scores = scores + dot_nt(stack, kv_own[c, :, 0].reshape(cols, width))
    scores = scores * (1.0 / math.sqrt(HEAD_DIM))
    here = iota((lines, tokens), 1) == (iota((lines, tokens), 0) >> head_shift) + row_first
    chain = chain_ref[...].astype(f32)
    residue = residue_ref[...]
    my_chain = jnp.sum(jnp.where(here, chain, 0.0), axis=1, keepdims=True)
    my_residue = jnp.sum(jnp.where(here, residue.astype(f32), 0.0), axis=1, keepdims=True)
    relation = rel[0]
    for c in range(1, n_col):
        relation = relation + rel[c]
    own_head = iota((lines, C), 1) == (iota((lines, C), 0) & (heads - 1))
    my_bias = jnp.sum(jnp.where(own_head, relation[0:1], 0.0), axis=1, keepdims=True)
    my_slope = jnp.sum(jnp.where(own_head, relation[1:2], 0.0), axis=1, keepdims=True)
    kind = iota((8, tokens), 0)
    facts = jnp.where(kind == 0, chain, jnp.where(kind == 1, (residue >> 4).astype(f32),
                                                  (residue & 15).astype(f32))).astype(bf16)
    take = (iota((tokens, cols), 0) == iota((tokens, cols), 1) + col_first).astype(f32).astype(bf16)
    facts = dot(facts, take)
    offset = my_residue - (facts[1:2] * 16.0 + facts[2:3])
    offset = jnp.clip(offset, -rel_reach, rel_reach) * (1.0 / rel_reach)
    scores = scores + jnp.where(my_chain == facts[0:1], my_bias + my_slope * offset, 0.0)
    real = (iota((lines, cols), 1) + col_first).astype(f32) < length

    def mix(chunk):
        part = None
        for s in range(share):
            term = (q_wide[chunk * share + s].astype(f32).reshape(rows, cols, C)
                    * col_full[chunk, s].astype(f32).reshape(1, cols, C))
            part = term if part is None else part + term
        return part

    mixed = mix(my_row)
    for d in far_first:
        ag_copies[d].wait_recv()
        mixed = mixed + mix(lax.rem(my_row + n_row - d, n_row))
    update = (gate * mixed.reshape(flat, C)).astype(bf16)
    pair = (pair.astype(f32) + dot(update, out_ref[1])).astype(bf16)
    pair_out_ref[...] = pair.reshape(rows, cols, C)
    store = pltpu.make_async_copy(pair_out_ref, pair_out_hbm, store_sem)
    store.start()

    normed = layer_norm(pair, bias_gain_ref[...]).astype(bf16).reshape(rows, cols, C)
    bias = [dot_nt(bias_proj_ref[...], normed[i]) for i in range(rows)]
    scores = scores + jnp.concatenate(bias, axis=0).astype(bf16).astype(f32)
    weights = jnp.where(real, jnp.exp(cap_value * jnp.tanh(scores * (1.0 / cap_value))), 0.0)
    bottom = jnp.sum(weights, axis=1, keepdims=True)
    weights = weights.astype(bf16)
    diagonal = iota((heads, C), 0) == iota((heads, C), 1)
    bottom = jnp.sum(jnp.where(diagonal[None], bottom.reshape(rows, heads, 1), 0.0), axis=1)
    bottom_high = bottom.astype(bf16)
    den_send[:, :C] = bottom_high
    den_send[:, C:] = (bottom - bottom_high.astype(f32)).astype(bf16)
    tops = []
    for c in range(n_col):
        attended = dot(weights, kv_own[c, :, 1].reshape(cols, width)).reshape(rows, heads, width)
        tops.append(jnp.sum(jnp.where(lanes_of[c][None], attended, 0.0), axis=1))
        num_send[c] = tops[c].astype(bf16)
    den_copies = push_cols(lambda d: den_send, lambda d: den_recv.at[d - 1], den_send_sem, den_recv_sem)
    num_copies = push_cols(lambda d: num_send, lambda d: num_recv.at[d - 1], num_send_sem, num_recv_sem)
    for copy in aout_copies:
        copy.wait_recv()
    deep = iota((2 * C, width), 0) & (C - 1)
    flat_lane = iota((2 * C, width), 1)
    wide_of = []
    for c in range(n_col):
        start = (deep - c * heads_here) * HEAD_DIM
        wide_of.append(((flat_lane >= start) & (flat_lane < start + HEAD_DIM)).astype(f32).astype(bf16))
    for d in range(1, n_col):
        den_copies[d - 1].wait_recv()
        bottom = bottom + (den_recv[d - 1, :, :C].astype(f32) + den_recv[d - 1, :, C:].astype(f32))
    inverse = jnp.where(iota((rows, C), 1) < heads, 1.0 / bottom, 0.0)
    inverse_high = inverse.astype(bf16)
    inverse = jnp.concatenate([inverse_high, (inverse - inverse_high.astype(f32)).astype(bf16)], axis=1)
    factors = [query_gates[c, 1].astype(f32) * dot(inverse, wide_of[c]) for c in range(n_col)]
    for copy in num_copies:
        copy.wait_recv()
    result = jnp.zeros((rows, width), f32)
    for c in range(n_col):
        top = tops[c]
        for d in range(1, n_col):
            top = top + num_recv[d - 1, c].astype(f32)
        result = result + dot((factors[c] * top).astype(bf16), aout_full[c])
    token_ref[...] = result.astype(bf16)
    store.wait()
    for copy in pushed:
        copy.wait_send()


def on_device(n_row, n_col, pair_act, single, token_mask, chain_index, residue_index, tri_gain, tri_qk,
              tri_vg, tri_out, bias_gain, bias_proj, chain_bias, pos_slope, attn_gain, attn_qk, attn_vg,
              attn_out):
    rows, cols, _ = pair_act.shape
    width = attn_qk.shape[2]
    share = TRI_DIM // n_row
    per = cols // rows
    by_col = [pltpu.SemaphoreType.DMA((n_col - 1,))] * 2
    by_row = [pltpu.SemaphoreType.DMA((n_row - 1,))] * 2
    vmem = pl.BlockSpec(memory_space=pltpu.VMEM)
    inputs = (
        pair_act, single, token_mask.reshape(1, -1), chain_index.reshape(1, -1),
        residue_index.reshape(1, -1), tri_gain, tri_qk, tri_vg, tri_out, bias_gain.reshape(1, -1),
        bias_proj.T, chain_bias.reshape(1, -1), pos_slope.reshape(1, -1), attn_gain.reshape(-1, C),
        jnp.swapaxes(attn_qk, 1, 2), jnp.swapaxes(attn_vg, 1, 2), attn_out,
    )
    return pl.pallas_call(
        functools.partial(kernel, n_row, n_col),
        out_shape=(
            jax.ShapeDtypeStruct(pair_act.shape, bf16),
            jax.ShapeDtypeStruct((rows, width), bf16),
        ),
        in_specs=[pl.BlockSpec(memory_space=pltpu.HBM)] * 17,
        out_specs=(pl.BlockSpec(memory_space=pltpu.HBM), vmem),
        scratch_shapes=[pltpu.VMEM(value.shape, value.dtype) for value in inputs[:1] + inputs] + [
            pltpu.VMEM((rows, TRI_DIM, C), bf16),
            pltpu.VMEM((n_col - 1, rows, TRI_DIM, C), bf16),
            pltpu.VMEM((n_row, share, cols, C), bf16),
            pltpu.VMEM((n_row - 1, share, cols, C), bf16),
            pltpu.VMEM((n_row, share, cols, C), bf16),
            pltpu.VMEM((TRI_DIM, rows * cols, C), bf16),
            pltpu.VMEM((n_row, 2, rows, width), bf16),
            pltpu.VMEM((n_col, per, 2, rows, width), bf16),
            pltpu.VMEM((n_col, 2, rows, width), bf16),
            pltpu.VMEM((n_col, 8, C), f32),
            pltpu.VMEM((n_col, width, width), bf16),
            pltpu.VMEM((n_col, width, width), bf16),
            pltpu.VMEM((n_col, rows, width), bf16),
            pltpu.VMEM((n_col - 1, n_col, rows, width), bf16),
            pltpu.VMEM((rows, 2 * C), bf16),
            pltpu.VMEM((n_col - 1, rows, 2 * C), bf16),
            pltpu.SemaphoreType.DMA((len(inputs),)),
            pltpu.SemaphoreType.DMA,
        ] + by_col + by_row + by_row + by_row + by_col * 6,
        compiler_params=pltpu.CompilerParams(
            collective_id=0, has_side_effects=True, vmem_limit_bytes=64 * 1024 * 1024
        ),
    )(*inputs)


def solution(mesh):
    return jax.shard_map(
        functools.partial(on_device, mesh.shape["row"], mesh.shape["col"]),
        mesh=mesh,
        in_specs=(
            P(("grp", "row"), "col", None),
            P(("grp", "row"), None),
            P("grp"),
            P("grp"),
            P("grp"),
            P(),
            P(),
            P(),
            P(),
            P(),
            P(),
            P("col"),
            P("col"),
            P(),
            P(None, None, "col"),
            P(None, None, "col"),
            P("col", None),
        ),
        out_specs=(P(("grp", "row"), "col", None), P(("grp", "row"), "col")),
        check_vma=False,
    )
```

```python
import functools
import math

import jax
import jax.numpy as jnp
from jax import lax
from jax.experimental import pallas as pl
from jax.experimental.pallas import tpu as pltpu
from jax.sharding import PartitionSpec as P

C = 128
TRI_HEADS = 8
TRI_DIM = 16
HEAD_DIM = 48

epsilon = 1e-05
cap_value = 10.0
rel_reach = 32.0
MESH = pl.DeviceIdType.MESH
f32 = jnp.float32
bf16 = jnp.bfloat16


def layer_norm(inputs, norm_gain):
    inputs = inputs.astype(f32)
    centered = inputs - jnp.mean(inputs, -1, keepdims=True)
    spread = jnp.mean(centered * centered, -1, keepdims=True)
    return centered * lax.rsqrt(spread + epsilon) * norm_gain


def feature(inputs):
    return jnp.where(inputs > 0, inputs + 1.0, jnp.exp(jnp.minimum(inputs, 0.0)))


def sigmoid(inputs):
    return 1.0 / (1.0 + jnp.exp(-inputs))


def dot(left, right):
    return jnp.dot(left, right, preferred_element_type=f32)


def dot_nt(left, right):
    return lax.dot_general(left, right, (((1,), (1,)), ((), ())), preferred_element_type=f32)


def dot_tn(left, right):
    return lax.dot_general(left, right, (((0,), (0,)), ((), ())), preferred_element_type=f32)


def iota(shape, dim):
    return lax.broadcasted_iota(jnp.int32, shape, dim)


def log2(number):
    power = number.bit_length() - 1
    assert 1 << power == number
    return power


def kernel(
    n_row,
    n_col,
    pair_hbm,
    single_hbm,
    mask_hbm,
    chain_hbm,
    residue_hbm,
    gain_hbm,
    qk_hbm,
    vg_hbm,
    out_hbm,
    bias_gain_hbm,
    bias_proj_hbm,
    chain_bias_hbm,
    slope_hbm,
    attn_gain_hbm,
    aqk_hbm,
    avg_hbm,
    aout_hbm,
    pair_out_hbm,
    token_ref,
    pair_out_ref,
    pair_ref,
    single_ref,
    mask_ref,
    chain_ref,
    residue_ref,
    gain_ref,
    qk_ref,
    vg_ref,
    out_ref,
    bias_gain_ref,
    bias_proj_ref,
    chain_bias_ref,
    slope_ref,
    attn_gain_ref,
    aqk_ref,
    avg_ref,
    aout_ref,
    row_part,
    row_recv,
    col_part,
    col_recv,
    col_full,
    q_wide,
    kv,
    kv_own,
    query_gates,
    rel,
    aout_send,
    aout_full,
    num_send,
    num_recv,
    den_send,
    den_recv,
    load_sem,
    store_sem,
    row_send_sem,
    row_recv_sem,
    rs_send_sem,
    rs_recv_sem,
    ag_send_sem,
    ag_recv_sem,
    kv_send_sem,
    kv_recv_sem,
    own_send_sem,
    own_recv_sem,
    qg_send_sem,
    qg_recv_sem,
    rel_send_sem,
    rel_recv_sem,
    aout_send_sem,
    aout_recv_sem,
    num_send_sem,
    num_recv_sem,
    den_send_sem,
    den_recv_sem,
):
    my_row = lax.axis_index("row")
    my_col = lax.axis_index("col")
    rows, cols, _ = pair_ref.shape
    tokens = mask_ref.shape[1]
    flat = rows * cols
    row_first = my_row * rows
    col_first = my_col * cols
    heads_here = chain_bias_ref.shape[1]
    heads = heads_here * n_col
    width = token_ref.shape[1]
    per = cols // rows
    tri_scale = 1.0 / (2.0 * TRI_DIM * math.sqrt(tokens))
    col_peers = [lax.rem(my_col + d, n_col) for d in range(n_col)]
    row_peers = [lax.rem(my_row + d, n_row) for d in range(n_row)]
    far_first = sorted(range(1, n_row), key=lambda d: abs(2 * d - n_row))
    pushed = []

    def push(src, dst, send_sem, recv_sem, where):
        copy = pltpu.make_async_remote_copy(
            src_ref=src, dst_ref=dst, send_sem=send_sem, recv_sem=recv_sem,
            device_id=where, device_id_type=MESH,
        )
        copy.start()
        pushed.append(copy)
        return copy

    def push_cols(src_of, dst_of, send_sem, recv_sem):
        copies = {
            d: push(src_of(d), dst_of(d), send_sem.at[d - 1], recv_sem.at[d - 1], {"col": col_peers[d]})
            for d in sorted(range(1, n_col), key=lambda d: abs(2 * d - n_col))
        }
        return [copies[d] for d in range(1, n_col)]

    loads = {}
    for position, (src, dst) in enumerate((
        (pair_hbm, pair_ref), (gain_hbm, gain_ref), (qk_hbm, qk_ref), (vg_hbm, vg_ref), (mask_hbm, mask_ref),
        (single_hbm, single_ref), (attn_gain_hbm, attn_gain_ref), (chain_bias_hbm, chain_bias_ref),
        (slope_hbm, slope_ref), (aqk_hbm, aqk_ref), (avg_hbm, avg_ref), (out_hbm, out_ref), (aout_hbm, aout_ref),
        (chain_hbm, chain_ref), (residue_hbm, residue_ref), (bias_gain_hbm, bias_gain_ref),
        (bias_proj_hbm, bias_proj_ref),
    )):
        loads[id(dst)] = pltpu.make_async_copy(src, dst, load_sem.at[position])
        loads[id(dst)].start()

    def loaded(*refs):
        for ref in refs:
            loads[id(ref)].wait()

    barrier = pltpu.get_barrier_semaphore()
    for d in range(1, n_col):
        pl.semaphore_signal(barrier, inc=1, device_id={"col": col_peers[d]}, device_id_type=MESH)
    for d in range(1, n_row):
        pl.semaphore_signal(barrier, inc=1, device_id={"row": row_peers[d]}, device_id_type=MESH)
    loaded(pair_ref, gain_ref, qk_ref, vg_ref, mask_ref)
    length = jnp.sum(mask_ref[...].astype(f32), axis=1, keepdims=True)

    half = rows // 2
    col_pos = (iota((1, cols, C), 1) + col_first).astype(f32)
    col_keep = col_pos < length.reshape(1, 1, 1)
    dim_shift = log2(TRI_DIM)
    left = iota((C, C), 0)
    right = iota((C, C), 1)
    same_head = (left >> dim_shift) == (right >> dim_shift)
    key_value_weight = jnp.concatenate([qk_ref[0, :, C:], vg_ref[0, :, :C]], axis=1)
    normed_halves = []
    row_copies = []
    for b in range(2):
        part = pair_ref[b * half:(b + 1) * half].reshape(half * cols, C)
        normed_halves.append(layer_norm(part, gain_ref[0:1, :]).astype(bf16))
        key_value = dot(normed_halves[b], key_value_weight)
        key_feat = jnp.where(col_keep, feature(key_value[:, :C]).reshape(half, cols, C), 0.0).astype(bf16)
        values = key_value[:, C:].astype(bf16).reshape(half, cols, C)
        for i in range(half):
            outer = jnp.where(same_head, dot_tn(key_feat[i], values[i]), 0.0)
            row_part[b * half + i] = jnp.sum(outer.reshape(TRI_HEADS, TRI_DIM, C), axis=0).astype(bf16)
        if b == 0:
            pl.semaphore_wait(barrier, n_row + n_col - 2)
        lines = pl.ds(b * half, half)
        row_copies.append(push_cols(lambda d: row_part.at[lines], lambda d: row_recv.at[d - 1, lines],
                                    row_send_sem.at[b], row_recv_sem.at[b]))

    loaded(single_ref, attn_gain_ref, chain_bias_ref, slope_ref)
    lane = iota((8, C), 1)
    top = iota((8, C), 0) == 0
    relation = jnp.zeros((8, C), f32)
    for h in range(heads_here):
        pick = jnp.where(top, chain_bias_ref[:, h:h + 1], slope_ref[:, h:h + 1])
        relation = relation + jnp.where(lane == my_col * heads_here + h, pick, 0.0)
    rel[my_col] = relation
    rel_copies = push_cols(lambda d: rel.at[my_col], lambda d: rel.at[my_col], rel_send_sem, rel_recv_sem)
    gains = [attn_gain_ref[g:g + 1, :] for g in range(attn_gain_ref.shape[0])]
    tok = layer_norm(single_ref[...], jnp.concatenate(gains, axis=1)).astype(bf16)
    loaded(aqk_ref, avg_ref)
    kv[my_row, 0] = dot_nt(tok, aqk_ref[1]).astype(bf16)
    kv[my_row, 1] = dot_nt(tok, avg_ref[0]).astype(bf16)
    kv_copies = {}
    for d in far_first:
        kv_copies[d] = push(kv.at[my_row], kv.at[my_row], kv_send_sem.at[d - 1],
                            kv_recv_sem.at[d - 1], {"row": row_peers[d]})
    query_gate_weight = jnp.concatenate([qk_ref[0, :, :C], vg_ref[0, :, C:]], axis=1)
    feat_halves = []
    gate_halves = []
    for b in range(2):
        query_gate = dot(normed_halves[b], query_gate_weight)
        feat_halves.append(feature(query_gate[:, :C]).astype(bf16).reshape(half, cols, C))
        gate_halves.append(sigmoid(query_gate[:, C:]) * tri_scale)
    query_gates[my_col, 0] = dot_nt(tok, aqk_ref[0]).astype(bf16)
    query_gates[my_col, 1] = sigmoid(dot_nt(tok, avg_ref[1])).astype(bf16)
    loaded(aout_ref)
    for c in range(n_col):
        aout_send[c] = aout_ref[:, c * width:(c + 1) * width]
    aout_full[my_col] = aout_send[my_col]

    loaded(out_ref, chain_ref, residue_ref, bias_gain_ref, bias_proj_ref)
    key_value_weight = jnp.concatenate([qk_ref[1, :, C:], vg_ref[1, :, :C]], axis=1)
    pairs, normed, key_feat, values = [], [], [], []
    for b in range(2):
        for copy in row_copies[b]:
            copy.wait_recv()
        lines = slice(b * half, (b + 1) * half)
        states = row_part[lines].astype(f32)
        for d in range(1, n_col):
            states = states + row_recv[d - 1, lines].astype(f32)
        states = states.astype(bf16)
        mixed = []
        for i in range(half):
            block = jnp.concatenate([states[i]] * TRI_HEADS, axis=0)
            block = jnp.where(same_head, block, jnp.zeros_like(block))
            mixed.append(dot(feat_halves[b][i], block))
        update = (gate_halves[b] * jnp.concatenate(mixed, axis=0)).astype(bf16)
        part = pair_ref[lines].reshape(half * cols, C).astype(f32)
        pairs.append((part + dot(update, out_ref[0])).astype(bf16))
        normed.append(layer_norm(pairs[b], gain_ref[1:2, :]).astype(bf16))
        key_value = dot(normed[b], key_value_weight)
        row_pos = (iota((half, 1, C), 0) + row_first + b * half).astype(f32)
        row_keep = row_pos < length.reshape(1, 1, 1)
        feat = jnp.where(row_keep, feature(key_value[:, :C]).reshape(half, cols, C), 0.0)
        key_feat.append(feat.astype(bf16).reshape(half * cols, C))
        values.append(key_value[:, C:])
    pair, normed, key_feat, values = [jnp.concatenate(both, axis=0)
                                      for both in (pairs, normed, key_feat, values)]
    qg_copies = push_cols(lambda d: query_gates.at[my_col], lambda d: query_gates.at[my_col],
                          qg_send_sem, qg_recv_sem)

    entry = jnp.where(same_head, left & (TRI_DIM - 1), -1)
    share = TRI_DIM // n_row

    def spread(first, count):
        parts = [(entry == first + s).astype(f32).astype(bf16) for s in range(count)]
        return parts[0] if count == 1 else jnp.concatenate(parts, axis=1)

    rs_copies = {}
    for d in far_first + [0]:
        owner = row_peers[d]
        wide = dot(key_feat, spread(owner * share, share))
        for s in range(share):
            part = wide[:, s * C:(s + 1) * C] * values
            col_part[owner, s] = jnp.sum(part.reshape(rows, cols, C), axis=0).astype(bf16)
        if d:
            rs_copies[d] = push(col_part.at[owner], col_recv.at[d - 1], rs_send_sem.at[d - 1],
                                rs_recv_sem.at[d - 1], {"row": owner})
    for d in far_first:
        kv_copies[d].wait_recv()
    kv_own[my_col] = kv[pl.ds(my_col * per, per)]
    own_copies = push_cols(lambda d: kv.at[pl.ds(col_peers[d] * per, per)], lambda d: kv_own.at[my_col],
                           own_send_sem, own_recv_sem)
    aout_copies = push_cols(lambda d: aout_send.at[col_peers[d]], lambda d: aout_full.at[my_col],
                            aout_send_sem, aout_recv_sem)
    query_gate = dot(normed, jnp.concatenate([qk_ref[1, :, :C], vg_ref[1, :, C:]], axis=1))
    query_feat = feature(query_gate[:, :C]).astype(bf16)
    gate = sigmoid(query_gate[:, C:]) * tri_scale
    for e in range(0, TRI_DIM, 2):
        wide = dot(query_feat, spread(e, 2)).astype(bf16)
        q_wide[e] = wide[:, :C]
        q_wide[e + 1] = wide[:, C:]
    total = col_part[my_row].astype(f32)
    for d in far_first:
        rs_copies[d].wait_recv()
        total = total + col_recv[d - 1].astype(f32)
    col_full[my_row] = total.astype(bf16)
    ag_copies = {}
    for d in far_first:
        ag_copies[d] = push(col_full.at[my_row], col_full.at[my_row], ag_send_sem.at[d - 1],
                            ag_recv_sem.at[d - 1], {"row": row_peers[d]})

    head_shift = log2(heads)
    lines = rows * heads
    for copy in rel_copies + qg_copies + own_copies:
        copy.wait_recv()
    head_of = iota((heads, width), 0)
    head_lane = iota((heads, width), 1)
    lanes_of = []
    for c in range(n_col):
        start = (head_of - c * heads_here) * HEAD_DIM
        lanes_of.append((head_lane >= start) & (head_lane < start + HEAD_DIM))
    scores = jnp.zeros((lines, cols), f32)
    for c in range(n_col):
        query = query_gates[c, 0].astype(f32)
        stack = jnp.where(lanes_of[c][None], query[:, None, :], 0.0).reshape(lines, width).astype(bf16)
        scores = scores + dot_nt(stack, kv_own[c, :, 0].reshape(cols, width))
    scores = scores * (1.0 / math.sqrt(HEAD_DIM))
    here = iota((lines, tokens), 1) == (iota((lines, tokens), 0) >> head_shift) + row_first
    chain = chain_ref[...].astype(f32)
    residue = residue_ref[...]
    my_chain = jnp.sum(jnp.where(here, chain, 0.0), axis=1, keepdims=True)
    my_residue = jnp.sum(jnp.where(here, residue.astype(f32), 0.0), axis=1, keepdims=True)
    relation = rel[0]
    for c in range(1, n_col):
        relation = relation + rel[c]
    own_head = iota((lines, C), 1) == (iota((lines, C), 0) & (heads - 1))
    my_bias = jnp.sum(jnp.where(own_head, relation[0:1], 0.0), axis=1, keepdims=True)
    my_slope = jnp.sum(jnp.where(own_head, relation[1:2], 0.0), axis=1, keepdims=True)
    kind = iota((8, tokens), 0)
    facts = jnp.where(kind == 0, chain, jnp.where(kind == 1, (residue >> 4).astype(f32),
                                                  (residue & 15).astype(f32))).astype(bf16)
    take = (iota((tokens, cols), 0) == iota((tokens, cols), 1) + col_first).astype(f32).astype(bf16)
    facts = dot(facts, take)
    offset = my_residue - (facts[1:2] * 16.0 + facts[2:3])
    offset = jnp.clip(offset, -rel_reach, rel_reach) * (1.0 / rel_reach)
    scores = scores + jnp.where(my_chain == facts[0:1], my_bias + my_slope * offset, 0.0)
    real = (iota((lines, cols), 1) + col_first).astype(f32) < length

    def mix(chunk):
        part = None
        for s in range(share):
            term = (q_wide[chunk * share + s].astype(f32).reshape(rows, cols, C)
                    * col_full[chunk, s].astype(f32).reshape(1, cols, C))
            part = term if part is None else part + term
        return part

    mixed = mix(my_row)
    for d in far_first:
        ag_copies[d].wait_recv()
        mixed = mixed + mix(lax.rem(my_row + n_row - d, n_row))
    update = (gate * mixed.reshape(flat, C)).astype(bf16)
    pair = (pair.astype(f32) + dot(update, out_ref[1])).astype(bf16)
    pair_out_ref[...] = pair.reshape(rows, cols, C)
    store = pltpu.make_async_copy(pair_out_ref, pair_out_hbm, store_sem)
    store.start()

    normed = layer_norm(pair, bias_gain_ref[...]).astype(bf16).reshape(rows, cols, C)
    bias = [dot_nt(bias_proj_ref[...], normed[i]) for i in range(rows)]
    scores = scores + jnp.concatenate(bias, axis=0).astype(bf16).astype(f32)
    weights = jnp.where(real, jnp.exp(cap_value * jnp.tanh(scores * (1.0 / cap_value))), 0.0)
    bottom = jnp.sum(weights, axis=1, keepdims=True)
    weights = weights.astype(bf16)
    diagonal = iota((heads, C), 0) == iota((heads, C), 1)
    bottom = jnp.sum(jnp.where(diagonal[None], bottom.reshape(rows, heads, 1), 0.0), axis=1)
    bottom_high = bottom.astype(bf16)
    den_send[:, :C] = bottom_high
    den_send[:, C:] = (bottom - bottom_high.astype(f32)).astype(bf16)
    tops = []
    for c in range(n_col):
        attended = dot(weights, kv_own[c, :, 1].reshape(cols, width)).reshape(rows, heads, width)
        tops.append(jnp.sum(jnp.where(lanes_of[c][None], attended, 0.0), axis=1))
        num_send[c] = tops[c].astype(bf16)
    den_copies = push_cols(lambda d: den_send, lambda d: den_recv.at[d - 1], den_send_sem, den_recv_sem)
    num_copies = push_cols(lambda d: num_send, lambda d: num_recv.at[d - 1], num_send_sem, num_recv_sem)
    for copy in aout_copies:
        copy.wait_recv()
    deep = iota((2 * C, width), 0) & (C - 1)
    flat_lane = iota((2 * C, width), 1)
    wide_of = []
    for c in range(n_col):
        start = (deep - c * heads_here) * HEAD_DIM
        wide_of.append(((flat_lane >= start) & (flat_lane < start + HEAD_DIM)).astype(f32).astype(bf16))
    for d in range(1, n_col):
        den_copies[d - 1].wait_recv()
        bottom = bottom + (den_recv[d - 1, :, :C].astype(f32) + den_recv[d - 1, :, C:].astype(f32))
    inverse = jnp.where(iota((rows, C), 1) < heads, 1.0 / bottom, 0.0)
    inverse_high = inverse.astype(bf16)
    inverse = jnp.concatenate([inverse_high, (inverse - inverse_high.astype(f32)).astype(bf16)], axis=1)
    factors = [query_gates[c, 1].astype(f32) * dot(inverse, wide_of[c]) for c in range(n_col)]
    for copy in num_copies:
        copy.wait_recv()
    result = jnp.zeros((rows, width), f32)
    for c in range(n_col):
        top = tops[c]
        for d in range(1, n_col):
            top = top + num_recv[d - 1, c].astype(f32)
        result = result + dot((factors[c] * top).astype(bf16), aout_full[c])
    token_ref[...] = result.astype(bf16)
    store.wait()
    for copy in pushed:
        copy.wait_send()


def store_kernel(pair_src, token_src, pair_dst, token_dst, sems):
    copies = [
        pltpu.make_async_copy(pair_src, pair_dst, sems.at[0]),
        pltpu.make_async_copy(token_src, token_dst, sems.at[1]),
    ]
    for copy in copies:
        copy.start()
    for copy in copies:
        copy.wait()


def on_device(n_row, n_col, pair_act, single, token_mask, chain_index, residue_index, tri_gain, tri_qk,
              tri_vg, tri_out, bias_gain, bias_proj, chain_bias, pos_slope, attn_gain, attn_qk, attn_vg,
              attn_out):
    rows, cols, _ = pair_act.shape
    width = attn_qk.shape[2]
    share = TRI_DIM // n_row
    per = cols // rows
    by_col = [pltpu.SemaphoreType.DMA((n_col - 1,))] * 2
    by_half = [pltpu.SemaphoreType.DMA((2, n_col - 1))] * 2
    by_row = [pltpu.SemaphoreType.DMA((n_row - 1,))] * 2
    vmem = pl.BlockSpec(memory_space=pltpu.VMEM)
    inputs = (
        pair_act, single, token_mask.reshape(1, -1), chain_index.reshape(1, -1),
        residue_index.reshape(1, -1), tri_gain, tri_qk, tri_vg, tri_out, bias_gain.reshape(1, -1),
        bias_proj.T, chain_bias.reshape(1, -1), pos_slope.reshape(1, -1), attn_gain.reshape(-1, C),
        jnp.swapaxes(attn_qk, 1, 2), jnp.swapaxes(attn_vg, 1, 2), attn_out,
    )
    out_shape = (jax.ShapeDtypeStruct(pair_act.shape, bf16), jax.ShapeDtypeStruct((rows, width), bf16))
    everything = 64 * 1024 * 1024
    results = pl.pallas_call(
        functools.partial(kernel, n_row, n_col),
        out_shape=out_shape,
        in_specs=[pl.BlockSpec(memory_space=pltpu.HBM)] * 17,
        out_specs=(pl.BlockSpec(memory_space=pltpu.HBM), vmem),
        scratch_shapes=[pltpu.VMEM(value.shape, value.dtype) for value in inputs[:1] + inputs] + [
            pltpu.VMEM((rows, TRI_DIM, C), bf16),
            pltpu.VMEM((n_col - 1, rows, TRI_DIM, C), bf16),
            pltpu.VMEM((n_row, share, cols, C), bf16),
            pltpu.VMEM((n_row - 1, share, cols, C), bf16),
            pltpu.VMEM((n_row, share, cols, C), bf16),
            pltpu.VMEM((TRI_DIM, rows * cols, C), bf16),
            pltpu.VMEM((n_row, 2, rows, width), bf16),
            pltpu.VMEM((n_col, per, 2, rows, width), bf16),
            pltpu.VMEM((n_col, 2, rows, width), bf16),
            pltpu.VMEM((n_col, 8, C), f32),
            pltpu.VMEM((n_col, width, width), bf16),
            pltpu.VMEM((n_col, width, width), bf16),
            pltpu.VMEM((n_col, rows, width), bf16),
            pltpu.VMEM((n_col - 1, n_col, rows, width), bf16),
            pltpu.VMEM((rows, 2 * C), bf16),
            pltpu.VMEM((n_col - 1, rows, 2 * C), bf16),
            pltpu.SemaphoreType.DMA((len(inputs),)),
            pltpu.SemaphoreType.DMA,
        ] + by_half + by_row + by_row + by_row + by_col * 6,
        compiler_params=pltpu.CompilerParams(
            collective_id=0, has_side_effects=True, vmem_limit_bytes=everything
        ),
    )(*inputs)
    return pl.pallas_call(
        store_kernel,
        out_shape=out_shape,
        in_specs=[pl.BlockSpec(memory_space=pltpu.HBM)] * 2,
        out_specs=[pl.BlockSpec(memory_space=pltpu.HBM)] * 2,
        scratch_shapes=[pltpu.SemaphoreType.DMA((2,))],
        compiler_params=pltpu.CompilerParams(vmem_limit_bytes=everything),
    )(*results)


def solution(mesh):
    return jax.shard_map(
        functools.partial(on_device, mesh.shape["row"], mesh.shape["col"]),
        mesh=mesh,
        in_specs=(
            P(("grp", "row"), "col", None),
            P(("grp", "row"), None),
            P("grp"),
            P("grp"),
            P("grp"),
            P(),
            P(),
            P(),
            P(),
            P(),
            P(),
            P("col"),
            P("col"),
            P(),
            P(None, None, "col"),
            P(None, None, "col"),
            P("col", None),
        ),
        out_specs=(P(("grp", "row"), "col", None), P(("grp", "row"), "col")),
        check_vma=False,
    )
```

```python
import functools
import math

import jax
import jax.numpy as jnp
from jax import lax
from jax.experimental import pallas as pl
from jax.experimental.pallas import tpu as pltpu
from jax.sharding import PartitionSpec as P

C = 128
TRI_HEADS = 8
TRI_DIM = 16
HEAD_DIM = 48

epsilon = 1e-05
cap_value = 10.0
rel_reach = 32.0
MESH = pl.DeviceIdType.MESH
f32 = jnp.float32
bf16 = jnp.bfloat16


def layer_norm(inputs, norm_gain):
    inputs = inputs.astype(f32)
    centered = inputs - jnp.mean(inputs, -1, keepdims=True)
    spread = jnp.mean(centered * centered, -1, keepdims=True)
    return centered * lax.rsqrt(spread + epsilon) * norm_gain


def feature(inputs):
    return jnp.where(inputs > 0, inputs + 1.0, jnp.exp(jnp.minimum(inputs, 0.0)))


def sigmoid(inputs):
    return 1.0 / (1.0 + jnp.exp(-inputs))


def dot(left, right):
    return jnp.dot(left, right, preferred_element_type=f32)


def dot_nt(left, right):
    return lax.dot_general(left, right, (((1,), (1,)), ((), ())), preferred_element_type=f32)


def dot_tn(left, right):
    return lax.dot_general(left, right, (((0,), (0,)), ((), ())), preferred_element_type=f32)


def iota(shape, dim):
    return lax.broadcasted_iota(jnp.int32, shape, dim)


def log2(number):
    power = number.bit_length() - 1
    assert 1 << power == number
    return power


def kernel(
    n_row,
    n_col,
    pair_hbm,
    single_hbm,
    mask_hbm,
    chain_hbm,
    residue_hbm,
    gain_hbm,
    qk_hbm,
    vg_hbm,
    out_hbm,
    bias_gain_hbm,
    bias_proj_hbm,
    chain_bias_hbm,
    slope_hbm,
    attn_gain_hbm,
    aqk_hbm,
    avg_hbm,
    aout_hbm,
    pair_out_hbm,
    token_ref,
    pair_out_ref,
    pair_ref,
    single_ref,
    mask_ref,
    chain_ref,
    residue_ref,
    gain_ref,
    qk_ref,
    vg_ref,
    out_ref,
    bias_gain_ref,
    bias_proj_ref,
    chain_bias_ref,
    slope_ref,
    attn_gain_ref,
    aqk_ref,
    avg_ref,
    aout_ref,
    row_part,
    row_recv,
    col_part,
    col_recv,
    col_full,
    q_wide,
    kv,
    kv_own,
    query_gates,
    rel,
    aout_send,
    aout_full,
    num_send,
    num_recv,
    load_sem,
    store_sem,
    row_send_sem,
    row_recv_sem,
    rs_send_sem,
    rs_recv_sem,
    ag_send_sem,
    ag_recv_sem,
    kv_send_sem,
    kv_recv_sem,
    own_send_sem,
    own_recv_sem,
    qg_send_sem,
    qg_recv_sem,
    rel_send_sem,
    rel_recv_sem,
    aout_send_sem,
    aout_recv_sem,
    num_send_sem,
    num_recv_sem,
):
    my_row = lax.axis_index("row")
    my_col = lax.axis_index("col")
    rows, cols, _ = pair_ref.shape
    tokens = mask_ref.shape[1]
    flat = rows * cols
    row_first = my_row * rows
    col_first = my_col * cols
    heads_here = chain_bias_ref.shape[1]
    heads = heads_here * n_col
    width = token_ref.shape[1]
    per = cols // rows
    tri_scale = 1.0 / (2.0 * TRI_DIM * math.sqrt(tokens))
    col_peers = [lax.rem(my_col + d, n_col) for d in range(n_col)]
    row_peers = [lax.rem(my_row + d, n_row) for d in range(n_row)]
    far_first = sorted(range(1, n_row), key=lambda d: abs(2 * d - n_row))
    pushed = []

    def push(src, dst, send_sem, recv_sem, where):
        copy = pltpu.make_async_remote_copy(
            src_ref=src, dst_ref=dst, send_sem=send_sem, recv_sem=recv_sem,
            device_id=where, device_id_type=MESH,
        )
        copy.start()
        pushed.append(copy)
        return copy

    def push_cols(src_of, dst_of, send_sem, recv_sem):
        copies = {
            d: push(src_of(d), dst_of(d), send_sem.at[d - 1], recv_sem.at[d - 1], {"col": col_peers[d]})
            for d in sorted(range(1, n_col), key=lambda d: abs(2 * d - n_col))
        }
        return [copies[d] for d in range(1, n_col)]

    loads = {}
    for position, (src, dst) in enumerate((
        (pair_hbm, pair_ref), (gain_hbm, gain_ref), (qk_hbm, qk_ref), (vg_hbm, vg_ref), (mask_hbm, mask_ref),
        (single_hbm, single_ref), (attn_gain_hbm, attn_gain_ref), (chain_bias_hbm, chain_bias_ref),
        (slope_hbm, slope_ref), (aqk_hbm, aqk_ref), (avg_hbm, avg_ref), (out_hbm, out_ref), (aout_hbm, aout_ref),
        (chain_hbm, chain_ref), (residue_hbm, residue_ref), (bias_gain_hbm, bias_gain_ref),
        (bias_proj_hbm, bias_proj_ref),
    )):
        loads[id(dst)] = pltpu.make_async_copy(src, dst, load_sem.at[position])
        loads[id(dst)].start()

    def loaded(*refs):
        for ref in refs:
            loads[id(ref)].wait()

    barrier = pltpu.get_barrier_semaphore()
    for d in range(1, n_col):
        pl.semaphore_signal(barrier, inc=1, device_id={"col": col_peers[d]}, device_id_type=MESH)
    for d in range(1, n_row):
        pl.semaphore_signal(barrier, inc=1, device_id={"row": row_peers[d]}, device_id_type=MESH)
    loaded(pair_ref, gain_ref, qk_ref, vg_ref, mask_ref)
    length = jnp.sum(mask_ref[...].astype(f32), axis=1, keepdims=True)

    half = rows // 2
    col_pos = (iota((1, cols, C), 1) + col_first).astype(f32)
    col_keep = col_pos < length.reshape(1, 1, 1)
    dim_shift = log2(TRI_DIM)
    left = iota((C, C), 0)
    right = iota((C, C), 1)
    same_head = (left >> dim_shift) == (right >> dim_shift)
    key_value_weight = jnp.concatenate([qk_ref[0, :, C:], vg_ref[0, :, :C]], axis=1)
    normed_halves = []
    row_copies = []
    for b in range(2):
        part = pair_ref[b * half:(b + 1) * half].reshape(half * cols, C)
        normed_halves.append(layer_norm(part, gain_ref[0:1, :]).astype(bf16))
        key_value = dot(normed_halves[b], key_value_weight)
        key_feat = jnp.where(col_keep, feature(key_value[:, :C]).reshape(half, cols, C), 0.0).astype(bf16)
        values = key_value[:, C:].astype(bf16).reshape(half, cols, C)
        for i in range(half):
            outer = jnp.where(same_head, dot_tn(key_feat[i], values[i]), 0.0)
            row_part[b * half + i] = jnp.sum(outer.reshape(TRI_HEADS, TRI_DIM, C), axis=0).astype(bf16)
        if b == 0:
            pl.semaphore_wait(barrier, n_row + n_col - 2)
        lines = pl.ds(b * half, half)
        row_copies.append(push_cols(lambda d: row_part.at[lines], lambda d: row_recv.at[d - 1, lines],
                                    row_send_sem.at[b], row_recv_sem.at[b]))

    loaded(single_ref, attn_gain_ref, chain_bias_ref, slope_ref)
    lane = iota((8, C), 1)
    top = iota((8, C), 0) == 0
    relation = jnp.zeros((8, C), f32)
    for h in range(heads_here):
        pick = jnp.where(top, chain_bias_ref[:, h:h + 1], slope_ref[:, h:h + 1])
        relation = relation + jnp.where(lane == my_col * heads_here + h, pick, 0.0)
    rel[my_col] = relation
    rel_copies = push_cols(lambda d: rel.at[my_col], lambda d: rel.at[my_col], rel_send_sem, rel_recv_sem)
    gains = [attn_gain_ref[g:g + 1, :] for g in range(attn_gain_ref.shape[0])]
    tok = layer_norm(single_ref[...], jnp.concatenate(gains, axis=1)).astype(bf16)
    loaded(aqk_ref, avg_ref)
    kv[my_row, 0] = dot_nt(tok, aqk_ref[1]).astype(bf16)
    kv[my_row, 1] = dot_nt(tok, avg_ref[0]).astype(bf16)
    kv_copies = {}
    for d in far_first:
        kv_copies[d] = push(kv.at[my_row], kv.at[my_row], kv_send_sem.at[d - 1],
                            kv_recv_sem.at[d - 1], {"row": row_peers[d]})
    query_gate_weight = jnp.concatenate([qk_ref[0, :, :C], vg_ref[0, :, C:]], axis=1)
    feat_halves = []
    gate_halves = []
    for b in range(2):
        query_gate = dot(normed_halves[b], query_gate_weight)
        feat_halves.append(feature(query_gate[:, :C]).astype(bf16).reshape(half, cols, C))
        gate_halves.append(sigmoid(query_gate[:, C:]) * tri_scale)
    query_gates[my_col, 0] = dot_nt(tok, aqk_ref[0]).astype(bf16)
    query_gates[my_col, 1] = sigmoid(dot_nt(tok, avg_ref[1])).astype(bf16)
    loaded(aout_ref)
    for c in range(n_col):
        aout_send[c] = aout_ref[:, c * width:(c + 1) * width]
    aout_full[my_col] = aout_send[my_col]
    aout_copies = push_cols(lambda d: aout_send.at[col_peers[d]], lambda d: aout_full.at[my_col],
                            aout_send_sem, aout_recv_sem)

    loaded(out_ref, chain_ref, residue_ref, bias_gain_ref, bias_proj_ref)
    key_value_weight = jnp.concatenate([qk_ref[1, :, C:], vg_ref[1, :, :C]], axis=1)
    pairs, normed, key_feat, values = [], [], [], []
    for b in range(2):
        for copy in row_copies[b]:
            copy.wait_recv()
        lines = slice(b * half, (b + 1) * half)
        states = row_part[lines].astype(f32)
        for d in range(1, n_col):
            states = states + row_recv[d - 1, lines].astype(f32)
        states = states.astype(bf16)
        mixed = []
        for i in range(half):
            block = jnp.concatenate([states[i]] * TRI_HEADS, axis=0)
            block = jnp.where(same_head, block, jnp.zeros_like(block))
            mixed.append(dot(feat_halves[b][i], block))
        update = (gate_halves[b] * jnp.concatenate(mixed, axis=0)).astype(bf16)
        part = pair_ref[lines].reshape(half * cols, C).astype(f32)
        pairs.append((part + dot(update, out_ref[0])).astype(bf16))
        normed.append(layer_norm(pairs[b], gain_ref[1:2, :]).astype(bf16))
        key_value = dot(normed[b], key_value_weight)
        row_pos = (iota((half, 1, C), 0) + row_first + b * half).astype(f32)
        row_keep = row_pos < length.reshape(1, 1, 1)
        feat = jnp.where(row_keep, feature(key_value[:, :C]).reshape(half, cols, C), 0.0)
        key_feat.append(feat.astype(bf16).reshape(half * cols, C))
        values.append(key_value[:, C:])
    pair, normed, key_feat, values = [jnp.concatenate(both, axis=0)
                                      for both in (pairs, normed, key_feat, values)]
    qg_copies = push_cols(lambda d: query_gates.at[my_col], lambda d: query_gates.at[my_col],
                          qg_send_sem, qg_recv_sem)

    entry = jnp.where(same_head, left & (TRI_DIM - 1), -1)
    share = TRI_DIM // n_row

    def spread(first, count):
        parts = [(entry == first + s).astype(f32).astype(bf16) for s in range(count)]
        return parts[0] if count == 1 else jnp.concatenate(parts, axis=1)

    rs_copies = {}
    for d in far_first + [0]:
        owner = row_peers[d]
        wide = dot(key_feat, spread(owner * share, share))
        for s in range(share):
            part = wide[:, s * C:(s + 1) * C] * values
            col_part[owner, s] = jnp.sum(part.reshape(rows, cols, C), axis=0).astype(bf16)
        if d:
            rs_copies[d] = push(col_part.at[owner], col_recv.at[d - 1], rs_send_sem.at[d - 1],
                                rs_recv_sem.at[d - 1], {"row": owner})
    for d in far_first:
        kv_copies[d].wait_recv()
    kv_own[my_col] = kv[pl.ds(my_col * per, per)]
    own_copies = push_cols(lambda d: kv.at[pl.ds(col_peers[d] * per, per)], lambda d: kv_own.at[my_col],
                           own_send_sem, own_recv_sem)
    query_gate = dot(normed, jnp.concatenate([qk_ref[1, :, :C], vg_ref[1, :, C:]], axis=1))
    query_feat = feature(query_gate[:, :C]).astype(bf16)
    gate = sigmoid(query_gate[:, C:]) * tri_scale
    for e in range(0, TRI_DIM, 2):
        wide = dot(query_feat, spread(e, 2)).astype(bf16)
        q_wide[e] = wide[:, :C]
        q_wide[e + 1] = wide[:, C:]
    total = col_part[my_row].astype(f32)
    for d in far_first:
        rs_copies[d].wait_recv()
        total = total + col_recv[d - 1].astype(f32)
    col_full[my_row] = total.astype(bf16)
    ag_copies = {}
    for d in far_first:
        ag_copies[d] = push(col_full.at[my_row], col_full.at[my_row], ag_send_sem.at[d - 1],
                            ag_recv_sem.at[d - 1], {"row": row_peers[d]})

    head_shift = log2(heads)
    lines = rows * heads
    for copy in rel_copies + qg_copies + own_copies:
        copy.wait_recv()
    head_of = iota((heads, width), 0)
    head_lane = iota((heads, width), 1)
    lanes_of = []
    for c in range(n_col):
        start = (head_of - c * heads_here) * HEAD_DIM
        lanes_of.append((head_lane >= start) & (head_lane < start + HEAD_DIM))
    scores = jnp.zeros((lines, cols), f32)
    for c in range(n_col):
        query = query_gates[c, 0].astype(f32)
        stack = jnp.where(lanes_of[c][None], query[:, None, :], 0.0).reshape(lines, width).astype(bf16)
        scores = scores + dot_nt(stack, kv_own[c, :, 0].reshape(cols, width))
    scores = scores * (1.0 / math.sqrt(HEAD_DIM))
    here = iota((lines, tokens), 1) == (iota((lines, tokens), 0) >> head_shift) + row_first
    chain = chain_ref[...].astype(f32)
    residue = residue_ref[...]
    my_chain = jnp.sum(jnp.where(here, chain, 0.0), axis=1, keepdims=True)
    my_residue = jnp.sum(jnp.where(here, residue.astype(f32), 0.0), axis=1, keepdims=True)
    relation = rel[0]
    for c in range(1, n_col):
        relation = relation + rel[c]
    own_head = iota((lines, C), 1) == (iota((lines, C), 0) & (heads - 1))
    my_bias = jnp.sum(jnp.where(own_head, relation[0:1], 0.0), axis=1, keepdims=True)
    my_slope = jnp.sum(jnp.where(own_head, relation[1:2], 0.0), axis=1, keepdims=True)
    kind = iota((8, tokens), 0)
    facts = jnp.where(kind == 0, chain, jnp.where(kind == 1, (residue >> 4).astype(f32),
                                                  (residue & 15).astype(f32))).astype(bf16)
    take = (iota((tokens, cols), 0) == iota((tokens, cols), 1) + col_first).astype(f32).astype(bf16)
    facts = dot(facts, take)
    offset = my_residue - (facts[1:2] * 16.0 + facts[2:3])
    offset = jnp.clip(offset, -rel_reach, rel_reach) * (1.0 / rel_reach)
    scores = scores + jnp.where(my_chain == facts[0:1], my_bias + my_slope * offset, 0.0)
    real = (iota((lines, cols), 1) + col_first).astype(f32) < length

    def mix(chunk):
        part = None
        for s in range(share):
            term = (q_wide[chunk * share + s].astype(f32).reshape(rows, cols, C)
                    * col_full[chunk, s].astype(f32).reshape(1, cols, C))
            part = term if part is None else part + term
        return part

    mixed = mix(my_row)
    for d in far_first:
        ag_copies[d].wait_recv()
        mixed = mixed + mix(lax.rem(my_row + n_row - d, n_row))
    update = (gate * mixed.reshape(flat, C)).astype(bf16)
    pair = (pair.astype(f32) + dot(update, out_ref[1])).astype(bf16)
    pair_out_ref[...] = pair.reshape(rows, cols, C)
    store = pltpu.make_async_copy(pair_out_ref, pair_out_hbm, store_sem)
    store.start()

    normed = layer_norm(pair, bias_gain_ref[...]).astype(bf16).reshape(rows, cols, C)
    bias = [dot_nt(bias_proj_ref[...], normed[i]) for i in range(rows)]
    scores = scores + jnp.concatenate(bias, axis=0).astype(bf16).astype(f32)
    weights = jnp.where(real, jnp.exp(cap_value * jnp.tanh(scores * (1.0 / cap_value))), 0.0)
    bottom = jnp.sum(weights, axis=1, keepdims=True)
    weights = weights.astype(bf16)
    lanes = num_send.shape[2]
    spare = lanes - width
    diagonal = iota((heads, spare), 0) == iota((heads, spare), 1)
    bottom = jnp.sum(jnp.where(diagonal[None], bottom.reshape(rows, heads, 1), 0.0), axis=1)
    bottom_high = bottom.astype(bf16).astype(f32)
    extras = [bottom_high, bottom - bottom_high] + [jnp.zeros((rows, spare), f32)] * (n_col - 2)
    tops = []
    for c in range(n_col):
        attended = dot(weights, kv_own[c, :, 1].reshape(cols, width)).reshape(rows, heads, width)
        tops.append(jnp.sum(jnp.where(lanes_of[c][None], attended, 0.0), axis=1))
        num_send[c] = jnp.concatenate([tops[c], extras[c]], axis=1).astype(bf16)
    num_copies = push_cols(lambda d: num_send, lambda d: num_recv.at[d - 1], num_send_sem, num_recv_sem)
    for copy in aout_copies:
        copy.wait_recv()
    deep = iota((spare, width), 0)
    flat_lane = iota((spare, width), 1)
    wide_of = []
    for c in range(n_col):
        start = (deep - c * heads_here) * HEAD_DIM
        wide_of.append(((flat_lane >= start) & (flat_lane < start + HEAD_DIM)).astype(f32).astype(bf16))
    for copy in pushed[:1 - n_col]:
        copy.wait_send()
    for copy in num_copies:
        copy.wait_recv()
    for c in range(n_col):
        for d in range(1, n_col):
            arrived = num_recv[d - 1, c].astype(f32)
            tops[c] = tops[c] + arrived[:, :width]
            if c < 2:
                bottom = bottom + arrived[:, width:]
    inverse = jnp.where(iota((rows, spare), 1) < heads, 1.0 / bottom, 0.0)
    inverse_high = inverse.astype(bf16)
    inverse_low = (inverse - inverse_high.astype(f32)).astype(bf16)
    result = jnp.zeros((rows, width), f32)
    for c in range(n_col):
        factor = query_gates[c, 1].astype(f32) * (dot(inverse_high, wide_of[c]) + dot(inverse_low, wide_of[c]))
        result = result + dot((factor * tops[c]).astype(bf16), aout_full[c])
    token_ref[...] = result.astype(bf16)
    store.wait()
    for copy in pushed[1 - n_col:]:
        copy.wait_send()


def on_device(n_row, n_col, pair_act, single, token_mask, chain_index, residue_index, tri_gain, tri_qk,
              tri_vg, tri_out, bias_gain, bias_proj, chain_bias, pos_slope, attn_gain, attn_qk, attn_vg,
              attn_out):
    rows, cols, _ = pair_act.shape
    width = attn_qk.shape[2]
    share = TRI_DIM // n_row
    per = cols // rows
    lanes = -(-width // C) * C
    by_col = [pltpu.SemaphoreType.DMA((n_col - 1,))] * 2
    by_half = [pltpu.SemaphoreType.DMA((2, n_col - 1))] * 2
    by_row = [pltpu.SemaphoreType.DMA((n_row - 1,))] * 2
    vmem = pl.BlockSpec(memory_space=pltpu.VMEM)
    inputs = (
        pair_act, single, token_mask.reshape(1, -1), chain_index.reshape(1, -1),
        residue_index.reshape(1, -1), tri_gain, tri_qk, tri_vg, tri_out, bias_gain.reshape(1, -1),
        bias_proj.T, chain_bias.reshape(1, -1), pos_slope.reshape(1, -1), attn_gain.reshape(-1, C),
        jnp.swapaxes(attn_qk, 1, 2), jnp.swapaxes(attn_vg, 1, 2), attn_out,
    )
    out_shape = (jax.ShapeDtypeStruct(pair_act.shape, bf16), jax.ShapeDtypeStruct((rows, width), bf16))
    everything = 64 * 1024 * 1024
    return pl.pallas_call(
        functools.partial(kernel, n_row, n_col),
        out_shape=out_shape,
        in_specs=[pl.BlockSpec(memory_space=pltpu.HBM)] * 17,
        out_specs=(pl.BlockSpec(memory_space=pltpu.HBM), vmem),
        scratch_shapes=[pltpu.VMEM(value.shape, value.dtype) for value in inputs[:1] + inputs] + [
            pltpu.VMEM((rows, TRI_DIM, C), bf16),
            pltpu.VMEM((n_col - 1, rows, TRI_DIM, C), bf16),
            pltpu.VMEM((n_row, share, cols, C), bf16),
            pltpu.VMEM((n_row - 1, share, cols, C), bf16),
            pltpu.VMEM((n_row, share, cols, C), bf16),
            pltpu.VMEM((TRI_DIM, rows * cols, C), bf16),
            pltpu.VMEM((n_row, 2, rows, width), bf16),
            pltpu.VMEM((n_col, per, 2, rows, width), bf16),
            pltpu.VMEM((n_col, 2, rows, width), bf16),
            pltpu.VMEM((n_col, 8, C), f32),
            pltpu.VMEM((n_col, width, width), bf16),
            pltpu.VMEM((n_col, width, width), bf16),
            pltpu.VMEM((n_col, rows, lanes), bf16),
            pltpu.VMEM((n_col - 1, n_col, rows, lanes), bf16),
            pltpu.SemaphoreType.DMA((len(inputs),)),
            pltpu.SemaphoreType.DMA,
        ] + by_half + by_row + by_row + by_row + by_col * 5,
        compiler_params=pltpu.CompilerParams(
            collective_id=0, has_side_effects=True, vmem_limit_bytes=everything
        ),
    )(*inputs)


def solution(mesh):
    return jax.shard_map(
        functools.partial(on_device, mesh.shape["row"], mesh.shape["col"]),
        mesh=mesh,
        in_specs=(
            P(("grp", "row"), "col", None),
            P(("grp", "row"), None),
            P("grp"),
            P("grp"),
            P("grp"),
            P(),
            P(),
            P(),
            P(),
            P(),
            P(),
            P("col"),
            P("col"),
            P(),
            P(None, None, "col"),
            P(None, None, "col"),
            P("col", None),
        ),
        out_specs=(P(("grp", "row"), "col", None), P(("grp", "row"), "col")),
        check_vma=False,
    )
```

```python
import functools
import math

import jax
import jax.numpy as jnp
from jax import lax
from jax.experimental import pallas as pl
from jax.experimental.pallas import tpu as pltpu
from jax.sharding import PartitionSpec as P

C = 128
TRI_HEADS = 8
TRI_DIM = 16
HEAD_DIM = 48

epsilon = 1e-05
cap_value = 10.0
rel_reach = 32.0
MESH = pl.DeviceIdType.MESH
f32 = jnp.float32
bf16 = jnp.bfloat16


def layer_norm(inputs, norm_gain):
    inputs = inputs.astype(f32)
    centered = inputs - jnp.mean(inputs, -1, keepdims=True)
    spread = jnp.mean(centered * centered, -1, keepdims=True)
    return centered * lax.rsqrt(spread + epsilon) * norm_gain


def feature(inputs):
    return jnp.where(inputs > 0, inputs + 1.0, jnp.exp(jnp.minimum(inputs, 0.0)))


def sigmoid(inputs):
    return 1.0 / (1.0 + jnp.exp(-inputs))


def dot(left, right):
    return jnp.dot(left, right, preferred_element_type=f32)


def dot_nt(left, right):
    return lax.dot_general(left, right, (((1,), (1,)), ((), ())), preferred_element_type=f32)


def dot_tn(left, right):
    return lax.dot_general(left, right, (((0,), (0,)), ((), ())), preferred_element_type=f32)


def iota(shape, dim):
    return lax.broadcasted_iota(jnp.int32, shape, dim)


def log2(number):
    power = number.bit_length() - 1
    assert 1 << power == number
    return power


def kernel(
    n_row,
    n_col,
    pair_hbm,
    single_hbm,
    mask_hbm,
    chain_hbm,
    residue_hbm,
    gain_hbm,
    qk_hbm,
    vg_hbm,
    out_hbm,
    bias_gain_hbm,
    bias_proj_hbm,
    chain_bias_hbm,
    slope_hbm,
    attn_gain_hbm,
    aqk_hbm,
    avg_hbm,
    aout_hbm,
    pair_out_hbm,
    token_ref,
    pair_out_ref,
    pair_ref,
    single_ref,
    mask_ref,
    chain_ref,
    residue_ref,
    gain_ref,
    qk_ref,
    vg_ref,
    out_ref,
    bias_gain_ref,
    bias_proj_ref,
    chain_bias_ref,
    slope_ref,
    attn_gain_ref,
    aqk_ref,
    avg_ref,
    aout_ref,
    row_part,
    row_recv,
    col_part,
    col_recv,
    col_full,
    q_wide,
    kv,
    kv_own,
    query_gates,
    rel,
    aout_send,
    aout_full,
    num_send,
    num_recv,
    load_sem,
    store_sem,
    row_send_sem,
    row_recv_sem,
    rs_send_sem,
    rs_recv_sem,
    ag_send_sem,
    ag_recv_sem,
    kv_send_sem,
    kv_recv_sem,
    own_send_sem,
    own_recv_sem,
    qg_send_sem,
    qg_recv_sem,
    rel_send_sem,
    rel_recv_sem,
    aout_send_sem,
    aout_recv_sem,
    num_send_sem,
    num_recv_sem,
):
    my_row = lax.axis_index("row")
    my_col = lax.axis_index("col")
    rows, cols, _ = pair_ref.shape
    tokens = mask_ref.shape[1]
    flat = rows * cols
    row_first = my_row * rows
    col_first = my_col * cols
    heads_here = chain_bias_ref.shape[1]
    heads = heads_here * n_col
    width = token_ref.shape[1]
    per = cols // rows
    tri_scale = 1.0 / (2.0 * TRI_DIM * math.sqrt(tokens))
    col_peers = [lax.rem(my_col + d, n_col) for d in range(n_col)]
    row_peers = [lax.rem(my_row + d, n_row) for d in range(n_row)]
    far_first = sorted(range(1, n_row), key=lambda d: abs(2 * d - n_row))
    pushed = []

    def push(src, dst, send_sem, recv_sem, where):
        copy = pltpu.make_async_remote_copy(
            src_ref=src, dst_ref=dst, send_sem=send_sem, recv_sem=recv_sem,
            device_id=where, device_id_type=MESH,
        )
        copy.start()
        pushed.append(copy)
        return copy

    def push_cols(src_of, dst_of, send_sem, recv_sem):
        copies = {
            d: push(src_of(d), dst_of(d), send_sem.at[d - 1], recv_sem.at[d - 1], {"col": col_peers[d]})
            for d in sorted(range(1, n_col), key=lambda d: abs(2 * d - n_col))
        }
        return [copies[d] for d in range(1, n_col)]

    loads = {}
    for position, (src, dst) in enumerate((
        (pair_hbm, pair_ref), (gain_hbm, gain_ref), (qk_hbm, qk_ref), (vg_hbm, vg_ref), (mask_hbm, mask_ref),
        (single_hbm, single_ref), (attn_gain_hbm, attn_gain_ref), (chain_bias_hbm, chain_bias_ref),
        (slope_hbm, slope_ref), (aqk_hbm, aqk_ref), (avg_hbm, avg_ref), (out_hbm, out_ref), (aout_hbm, aout_ref),
        (chain_hbm, chain_ref), (residue_hbm, residue_ref), (bias_gain_hbm, bias_gain_ref),
        (bias_proj_hbm, bias_proj_ref),
    )):
        loads[id(dst)] = pltpu.make_async_copy(src, dst, load_sem.at[position])
        loads[id(dst)].start()

    def loaded(*refs):
        for ref in refs:
            loads[id(ref)].wait()

    barrier = pltpu.get_barrier_semaphore()
    for d in range(1, n_col):
        pl.semaphore_signal(barrier, inc=1, device_id={"col": col_peers[d]}, device_id_type=MESH)
    for d in range(1, n_row):
        pl.semaphore_signal(barrier, inc=1, device_id={"row": row_peers[d]}, device_id_type=MESH)
    loaded(pair_ref, gain_ref, qk_ref, vg_ref, mask_ref)
    length = jnp.sum(mask_ref[...].astype(f32), axis=1, keepdims=True)

    half = rows // 2
    col_pos = (iota((1, cols, C), 1) + col_first).astype(f32)
    col_keep = col_pos < length.reshape(1, 1, 1)
    dim_shift = log2(TRI_DIM)
    left = iota((C, C), 0)
    right = iota((C, C), 1)
    same_head = (left >> dim_shift) == (right >> dim_shift)
    key_value_weight = jnp.concatenate([qk_ref[0, :, C:], vg_ref[0, :, :C]], axis=1)
    normed_halves = []
    row_copies = []
    for b in range(2):
        part = pair_ref[b * half:(b + 1) * half].reshape(half * cols, C)
        normed_halves.append(layer_norm(part, gain_ref[0:1, :]).astype(bf16))
        key_value = dot(normed_halves[b], key_value_weight)
        key_feat = jnp.where(col_keep, feature(key_value[:, :C]).reshape(half, cols, C), 0.0).astype(bf16)
        values = key_value[:, C:].astype(bf16).reshape(half, cols, C)
        for i in range(half):
            outer = jnp.where(same_head, dot_tn(key_feat[i], values[i]), 0.0)
            row_part[b * half + i] = jnp.sum(outer.reshape(TRI_HEADS, TRI_DIM, C), axis=0).astype(bf16)
        if b == 0:
            pl.semaphore_wait(barrier, n_row + n_col - 2)
        lines = pl.ds(b * half, half)
        row_copies.append(push_cols(lambda d: row_part.at[lines], lambda d: row_recv.at[d - 1, lines],
                                    row_send_sem.at[b], row_recv_sem.at[b]))

    loaded(single_ref, attn_gain_ref, chain_bias_ref, slope_ref)
    lane = iota((8, C), 1)
    top = iota((8, C), 0) == 0
    relation = jnp.zeros((8, C), f32)
    for h in range(heads_here):
        pick = jnp.where(top, chain_bias_ref[:, h:h + 1], slope_ref[:, h:h + 1])
        relation = relation + jnp.where(lane == my_col * heads_here + h, pick, 0.0)
    rel[my_col] = relation
    rel_copies = push_cols(lambda d: rel.at[my_col], lambda d: rel.at[my_col], rel_send_sem, rel_recv_sem)
    gains = [attn_gain_ref[g:g + 1, :] for g in range(attn_gain_ref.shape[0])]
    tok = layer_norm(single_ref[...], jnp.concatenate(gains, axis=1)).astype(bf16)
    loaded(aqk_ref, avg_ref)
    kv[my_row, 0] = dot_nt(tok, aqk_ref[1]).astype(bf16)
    kv[my_row, 1] = dot_nt(tok, avg_ref[0]).astype(bf16)
    kv_copies = {}
    for d in far_first:
        kv_copies[d] = push(kv.at[my_row], kv.at[my_row], kv_send_sem.at[d - 1],
                            kv_recv_sem.at[d - 1], {"row": row_peers[d]})
    query_gate_weight = jnp.concatenate([qk_ref[0, :, :C], vg_ref[0, :, C:]], axis=1)
    feat_halves = []
    gate_halves = []
    for b in range(2):
        query_gate = dot(normed_halves[b], query_gate_weight)
        feat_halves.append(feature(query_gate[:, :C]).astype(bf16).reshape(half, cols, C))
        gate_halves.append(sigmoid(query_gate[:, C:]) * tri_scale)
    query_gates[my_col, 0] = dot_nt(tok, aqk_ref[0]).astype(bf16)
    query_gates[my_col, 1] = sigmoid(dot_nt(tok, avg_ref[1])).astype(bf16)
    loaded(aout_ref)
    for c in range(n_col):
        aout_send[c] = aout_ref[:, c * width:(c + 1) * width]
    aout_full[my_col] = aout_send[my_col]

    loaded(out_ref, chain_ref, residue_ref, bias_gain_ref, bias_proj_ref)
    key_value_weight = jnp.concatenate([qk_ref[1, :, C:], vg_ref[1, :, :C]], axis=1)
    pairs, normed, key_feat, values = [], [], [], []
    for b in range(2):
        for copy in row_copies[b]:
            copy.wait_recv()
        lines = slice(b * half, (b + 1) * half)
        states = row_part[lines].astype(f32)
        for d in range(1, n_col):
            states = states + row_recv[d - 1, lines].astype(f32)
        states = states.astype(bf16)
        mixed = []
        for i in range(half):
            block = jnp.concatenate([states[i]] * TRI_HEADS, axis=0)
            block = jnp.where(same_head, block, jnp.zeros_like(block))
            mixed.append(dot(feat_halves[b][i], block))
        update = (gate_halves[b] * jnp.concatenate(mixed, axis=0)).astype(bf16)
        part = pair_ref[lines].reshape(half * cols, C).astype(f32)
        pairs.append((part + dot(update, out_ref[0])).astype(bf16))
        normed.append(layer_norm(pairs[b], gain_ref[1:2, :]).astype(bf16))
        key_value = dot(normed[b], key_value_weight)
        row_pos = (iota((half, 1, C), 0) + row_first + b * half).astype(f32)
        row_keep = row_pos < length.reshape(1, 1, 1)
        feat = jnp.where(row_keep, feature(key_value[:, :C]).reshape(half, cols, C), 0.0)
        key_feat.append(feat.astype(bf16).reshape(half * cols, C))
        values.append(key_value[:, C:])
    pair, normed, key_feat, values = [jnp.concatenate(both, axis=0)
                                      for both in (pairs, normed, key_feat, values)]
    qg_copies = push_cols(lambda d: query_gates.at[my_col], lambda d: query_gates.at[my_col],
                          qg_send_sem, qg_recv_sem)

    entry = jnp.where(same_head, left & (TRI_DIM - 1), -1)
    share = TRI_DIM // n_row

    def spread(first, count):
        parts = [(entry == first + s).astype(f32).astype(bf16) for s in range(count)]
        return parts[0] if count == 1 else jnp.concatenate(parts, axis=1)

    rs_copies = {}
    for d in far_first + [0]:
        owner = row_peers[d]
        wide = dot(key_feat, spread(owner * share, share))
        for s in range(share):
            part = wide[:, s * C:(s + 1) * C] * values
            col_part[owner, s] = jnp.sum(part.reshape(rows, cols, C), axis=0).astype(bf16)
        if d:
            rs_copies[d] = push(col_part.at[owner], col_recv.at[d - 1], rs_send_sem.at[d - 1],
                                rs_recv_sem.at[d - 1], {"row": owner})
    for d in far_first:
        kv_copies[d].wait_recv()
    kv_own[my_col] = kv[pl.ds(my_col * per, per)]
    own_copies = push_cols(lambda d: kv.at[pl.ds(col_peers[d] * per, per)], lambda d: kv_own.at[my_col],
                           own_send_sem, own_recv_sem)
    query_gate = dot(normed, jnp.concatenate([qk_ref[1, :, :C], vg_ref[1, :, C:]], axis=1))
    query_feat = feature(query_gate[:, :C]).astype(bf16)
    gate = sigmoid(query_gate[:, C:]) * tri_scale
    for e in range(0, TRI_DIM, 2):
        wide = dot(query_feat, spread(e, 2)).astype(bf16)
        q_wide[e] = wide[:, :C]
        q_wide[e + 1] = wide[:, C:]
    total = col_part[my_row].astype(f32)
    for d in far_first:
        rs_copies[d].wait_recv()
        total = total + col_recv[d - 1].astype(f32)
    col_full[my_row] = total.astype(bf16)
    ag_copies = {}
    for d in far_first:
        ag_copies[d] = push(col_full.at[my_row], col_full.at[my_row], ag_send_sem.at[d - 1],
                            ag_recv_sem.at[d - 1], {"row": row_peers[d]})

    aout_copies = push_cols(lambda d: aout_send.at[col_peers[d]], lambda d: aout_full.at[my_col],
                            aout_send_sem, aout_recv_sem)

    head_shift = log2(heads)
    lines = rows * heads
    for copy in rel_copies + qg_copies + own_copies:
        copy.wait_recv()
    head_of = iota((heads, width), 0)
    head_lane = iota((heads, width), 1)
    lanes_of = []
    for c in range(n_col):
        start = (head_of - c * heads_here) * HEAD_DIM
        lanes_of.append((head_lane >= start) & (head_lane < start + HEAD_DIM))
    scores = jnp.zeros((lines, cols), f32)
    for c in range(n_col):
        query = query_gates[c, 0].astype(f32)
        stack = jnp.where(lanes_of[c][None], query[:, None, :], 0.0).reshape(lines, width).astype(bf16)
        scores = scores + dot_nt(stack, kv_own[c, :, 0].reshape(cols, width))
    scores = scores * (1.0 / math.sqrt(HEAD_DIM))
    here = iota((lines, tokens), 1) == (iota((lines, tokens), 0) >> head_shift) + row_first
    chain = chain_ref[...].astype(f32)
    residue = residue_ref[...]
    my_chain = jnp.sum(jnp.where(here, chain, 0.0), axis=1, keepdims=True)
    my_residue = jnp.sum(jnp.where(here, residue.astype(f32), 0.0), axis=1, keepdims=True)
    relation = rel[0]
    for c in range(1, n_col):
        relation = relation + rel[c]
    own_head = iota((lines, C), 1) == (iota((lines, C), 0) & (heads - 1))
    my_bias = jnp.sum(jnp.where(own_head, relation[0:1], 0.0), axis=1, keepdims=True)
    my_slope = jnp.sum(jnp.where(own_head, relation[1:2], 0.0), axis=1, keepdims=True)
    kind = iota((8, tokens), 0)
    facts = jnp.where(kind == 0, chain, jnp.where(kind == 1, (residue >> 4).astype(f32),
                                                  (residue & 15).astype(f32))).astype(bf16)
    take = (iota((tokens, cols), 0) == iota((tokens, cols), 1) + col_first).astype(f32).astype(bf16)
    facts = dot(facts, take)
    offset = my_residue - (facts[1:2] * 16.0 + facts[2:3])
    offset = jnp.clip(offset, -rel_reach, rel_reach) * (1.0 / rel_reach)
    scores = scores + jnp.where(my_chain == facts[0:1], my_bias + my_slope * offset, 0.0)
    real = (iota((lines, cols), 1) + col_first).astype(f32) < length

    def mix(chunk):
        part = None
        for s in range(share):
            term = (q_wide[chunk * share + s].astype(f32).reshape(rows, cols, C)
                    * col_full[chunk, s].astype(f32).reshape(1, cols, C))
            part = term if part is None else part + term
        return part

    mixed = mix(my_row)
    for d in far_first:
        ag_copies[d].wait_recv()
        mixed = mixed + mix(lax.rem(my_row + n_row - d, n_row))
    update = (gate * mixed.reshape(flat, C)).astype(bf16)
    pair = (pair.astype(f32) + dot(update, out_ref[1])).astype(bf16)
    pair_out_ref[...] = pair.reshape(rows, cols, C)
    store = pltpu.make_async_copy(pair_out_ref, pair_out_hbm, store_sem)
    store.start()

    normed = layer_norm(pair, bias_gain_ref[...]).astype(bf16).reshape(rows, cols, C)
    bias = [dot_nt(bias_proj_ref[...], normed[i]) for i in range(rows)]
    scores = scores + jnp.concatenate(bias, axis=0).astype(bf16).astype(f32)
    weights = jnp.where(real, jnp.exp(cap_value * jnp.tanh(scores * (1.0 / cap_value))), 0.0)
    bottom = jnp.sum(weights, axis=1, keepdims=True)
    weights = weights.astype(bf16)
    lanes = num_send.shape[2]
    spare = lanes - width
    diagonal = iota((heads, spare), 0) == iota((heads, spare), 1)
    bottom = jnp.sum(jnp.where(diagonal[None], bottom.reshape(rows, heads, 1), 0.0), axis=1)
    bottom_high = bottom.astype(bf16).astype(f32)
    extras = [bottom_high, bottom - bottom_high] + [jnp.zeros((rows, spare), f32)] * (n_col - 2)
    tops = []
    for c in range(n_col):
        attended = dot(weights, kv_own[c, :, 1].reshape(cols, width)).reshape(rows, heads, width)
        tops.append(jnp.sum(jnp.where(lanes_of[c][None], attended, 0.0), axis=1))
        num_send[c] = jnp.concatenate([tops[c], extras[c]], axis=1).astype(bf16)
    num_copies = push_cols(lambda d: num_send, lambda d: num_recv.at[d - 1], num_send_sem, num_recv_sem)
    for copy in aout_copies:
        copy.wait_recv()
    deep = iota((spare, width), 0)
    flat_lane = iota((spare, width), 1)
    wide_of = []
    for c in range(n_col):
        start = (deep - c * heads_here) * HEAD_DIM
        wide_of.append(((flat_lane >= start) & (flat_lane < start + HEAD_DIM)).astype(f32).astype(bf16))
    for copy in pushed[:1 - n_col]:
        copy.wait_send()
    for copy in num_copies:
        copy.wait_recv()
    for c in range(n_col):
        for d in range(1, n_col):
            arrived = num_recv[d - 1, c].astype(f32)
            tops[c] = tops[c] + arrived[:, :width]
            if c < 2:
                bottom = bottom + arrived[:, width:]
    inverse = jnp.where(iota((rows, spare), 1) < heads, 1.0 / bottom, 0.0)
    inverse_high = inverse.astype(bf16)
    inverse_low = (inverse - inverse_high.astype(f32)).astype(bf16)
    result = jnp.zeros((rows, width), f32)
    for c in range(n_col):
        factor = query_gates[c, 1].astype(f32) * (dot(inverse_high, wide_of[c]) + dot(inverse_low, wide_of[c]))
        result = result + dot((factor * tops[c]).astype(bf16), aout_full[c])
    token_ref[...] = result.astype(bf16)
    store.wait()
    for copy in pushed[1 - n_col:]:
        copy.wait_send()


def on_device(n_row, n_col, pair_act, single, token_mask, chain_index, residue_index, tri_gain, tri_qk,
              tri_vg, tri_out, bias_gain, bias_proj, chain_bias, pos_slope, attn_gain, attn_qk, attn_vg,
              attn_out):
    rows, cols, _ = pair_act.shape
    width = attn_qk.shape[2]
    share = TRI_DIM // n_row
    per = cols // rows
    lanes = -(-width // C) * C
    by_col = [pltpu.SemaphoreType.DMA((n_col - 1,))] * 2
    by_half = [pltpu.SemaphoreType.DMA((2, n_col - 1))] * 2
    by_row = [pltpu.SemaphoreType.DMA((n_row - 1,))] * 2
    vmem = pl.BlockSpec(memory_space=pltpu.VMEM)
    inputs = (
        pair_act, single, token_mask.reshape(1, -1), chain_index.reshape(1, -1),
        residue_index.reshape(1, -1), tri_gain, tri_qk, tri_vg, tri_out, bias_gain.reshape(1, -1),
        bias_proj.T, chain_bias.reshape(1, -1), pos_slope.reshape(1, -1), attn_gain.reshape(-1, C),
        jnp.swapaxes(attn_qk, 1, 2), jnp.swapaxes(attn_vg, 1, 2), attn_out,
    )
    out_shape = (jax.ShapeDtypeStruct(pair_act.shape, bf16), jax.ShapeDtypeStruct((rows, width), bf16))
    everything = 64 * 1024 * 1024
    return pl.pallas_call(
        functools.partial(kernel, n_row, n_col),
        out_shape=out_shape,
        in_specs=[pl.BlockSpec(memory_space=pltpu.HBM)] * 17,
        out_specs=(pl.BlockSpec(memory_space=pltpu.HBM), vmem),
        scratch_shapes=[pltpu.VMEM(value.shape, value.dtype) for value in inputs[:1] + inputs] + [
            pltpu.VMEM((rows, TRI_DIM, C), bf16),
            pltpu.VMEM((n_col - 1, rows, TRI_DIM, C), bf16),
            pltpu.VMEM((n_row, share, cols, C), bf16),
            pltpu.VMEM((n_row - 1, share, cols, C), bf16),
            pltpu.VMEM((n_row, share, cols, C), bf16),
            pltpu.VMEM((TRI_DIM, rows * cols, C), bf16),
            pltpu.VMEM((n_row, 2, rows, width), bf16),
            pltpu.VMEM((n_col, per, 2, rows, width), bf16),
            pltpu.VMEM((n_col, 2, rows, width), bf16),
            pltpu.VMEM((n_col, 8, C), f32),
            pltpu.VMEM((n_col, width, width), bf16),
            pltpu.VMEM((n_col, width, width), bf16),
            pltpu.VMEM((n_col, rows, lanes), bf16),
            pltpu.VMEM((n_col - 1, n_col, rows, lanes), bf16),
            pltpu.SemaphoreType.DMA((len(inputs),)),
            pltpu.SemaphoreType.DMA,
        ] + by_half + by_row + by_row + by_row + by_col * 5,
        compiler_params=pltpu.CompilerParams(
            collective_id=0, has_side_effects=True, vmem_limit_bytes=everything
        ),
    )(*inputs)


def solution(mesh):
    return jax.shard_map(
        functools.partial(on_device, mesh.shape["row"], mesh.shape["col"]),
        mesh=mesh,
        in_specs=(
            P(("grp", "row"), "col", None),
            P(("grp", "row"), None),
            P("grp"),
            P("grp"),
            P("grp"),
            P(),
            P(),
            P(),
            P(),
            P(),
            P(),
            P("col"),
            P("col"),
            P(),
            P(None, None, "col"),
            P(None, None, "col"),
            P("col", None),
        ),
        out_specs=(P(("grp", "row"), "col", None), P(("grp", "row"), "col")),
        check_vma=False,
    )
```

```python
import functools
import math

import jax
import jax.numpy as jnp
from jax import lax
from jax.experimental import pallas as pl
from jax.experimental.pallas import tpu as pltpu
from jax.sharding import PartitionSpec as P

C = 128
TRI_HEADS = 8
TRI_DIM = 16
HEAD_DIM = 48

epsilon = 1e-05
cap_value = 10.0
rel_reach = 32.0
MESH = pl.DeviceIdType.MESH
f32 = jnp.float32
bf16 = jnp.bfloat16


def layer_norm(inputs, norm_gain):
    inputs = inputs.astype(f32)
    centered = inputs - jnp.mean(inputs, -1, keepdims=True)
    spread = jnp.mean(centered * centered, -1, keepdims=True)
    return centered * lax.rsqrt(spread + epsilon) * norm_gain


def feature(inputs):
    return jnp.where(inputs > 0, inputs + 1.0, jnp.exp(jnp.minimum(inputs, 0.0)))


def sigmoid(inputs):
    return 1.0 / (1.0 + jnp.exp(-inputs))


def dot(left, right):
    return jnp.dot(left, right, preferred_element_type=f32)


def dot_nt(left, right):
    return lax.dot_general(left, right, (((1,), (1,)), ((), ())), preferred_element_type=f32)


def dot_tn(left, right):
    return lax.dot_general(left, right, (((0,), (0,)), ((), ())), preferred_element_type=f32)


def iota(shape, dim):
    return lax.broadcasted_iota(jnp.int32, shape, dim)


def log2(number):
    power = number.bit_length() - 1
    assert 1 << power == number
    return power


def kernel(
    n_row,
    n_col,
    pair_hbm,
    single_hbm,
    mask_hbm,
    chain_hbm,
    residue_hbm,
    gain_hbm,
    qk_hbm,
    vg_hbm,
    out_hbm,
    bias_gain_hbm,
    bias_proj_hbm,
    chain_bias_hbm,
    slope_hbm,
    attn_gain_hbm,
    aqk_hbm,
    avg_hbm,
    aout_hbm,
    pair_out_hbm,
    token_ref,
    pair_out_ref,
    pair_ref,
    single_ref,
    mask_ref,
    chain_ref,
    residue_ref,
    gain_ref,
    qk_ref,
    vg_ref,
    out_ref,
    bias_gain_ref,
    bias_proj_ref,
    chain_bias_ref,
    slope_ref,
    attn_gain_ref,
    aqk_ref,
    avg_ref,
    aout_ref,
    row_part,
    row_recv,
    col_part,
    col_recv,
    col_full,
    q_wide,
    kv,
    kv_own,
    query_gates,
    rel,
    aout_send,
    aout_full,
    num_send,
    num_recv,
    load_sem,
    store_sem,
    row_send_sem,
    row_recv_sem,
    rs_send_sem,
    rs_recv_sem,
    ag_send_sem,
    ag_recv_sem,
    kv_send_sem,
    kv_recv_sem,
    own_send_sem,
    own_recv_sem,
    qg_send_sem,
    qg_recv_sem,
    rel_send_sem,
    rel_recv_sem,
    aout_send_sem,
    aout_recv_sem,
    num_send_sem,
    num_recv_sem,
):
    my_row = lax.axis_index("row")
    my_col = lax.axis_index("col")
    rows, cols, _ = pair_ref.shape
    tokens = mask_ref.shape[1]
    flat = rows * cols
    row_first = my_row * rows
    col_first = my_col * cols
    heads_here = chain_bias_ref.shape[1]
    heads = heads_here * n_col
    width = token_ref.shape[1]
    per = cols // rows
    tri_scale = 1.0 / (2.0 * TRI_DIM * math.sqrt(tokens))
    col_peers = [lax.rem(my_col + d, n_col) for d in range(n_col)]
    row_peers = [lax.rem(my_row + d, n_row) for d in range(n_row)]
    far_first = sorted(range(1, n_row), key=lambda d: abs(2 * d - n_row))
    pushed = []

    def push(src, dst, send_sem, recv_sem, where):
        copy = pltpu.make_async_remote_copy(
            src_ref=src, dst_ref=dst, send_sem=send_sem, recv_sem=recv_sem,
            device_id=where, device_id_type=MESH,
        )
        copy.start()
        pushed.append(copy)
        return copy

    def push_cols(src_of, dst_of, send_sem, recv_sem):
        copies = {
            d: push(src_of(d), dst_of(d), send_sem.at[d - 1], recv_sem.at[d - 1], {"col": col_peers[d]})
            for d in sorted(range(1, n_col), key=lambda d: abs(2 * d - n_col))
        }
        return [copies[d] for d in range(1, n_col)]

    loads = {}
    for position, (src, dst) in enumerate((
        (pair_hbm, pair_ref), (gain_hbm, gain_ref), (qk_hbm, qk_ref), (vg_hbm, vg_ref), (mask_hbm, mask_ref),
        (single_hbm, single_ref), (attn_gain_hbm, attn_gain_ref), (chain_bias_hbm, chain_bias_ref),
        (slope_hbm, slope_ref), (aqk_hbm, aqk_ref), (avg_hbm, avg_ref), (out_hbm, out_ref), (aout_hbm, aout_ref),
        (chain_hbm, chain_ref), (residue_hbm, residue_ref), (bias_gain_hbm, bias_gain_ref),
        (bias_proj_hbm, bias_proj_ref),
    )):
        loads[id(dst)] = pltpu.make_async_copy(src, dst, load_sem.at[position])
        loads[id(dst)].start()

    def loaded(*refs):
        for ref in refs:
            loads[id(ref)].wait()

    barrier = pltpu.get_barrier_semaphore()
    for d in range(1, n_col):
        pl.semaphore_signal(barrier, inc=1, device_id={"col": col_peers[d]}, device_id_type=MESH)
    for d in range(1, n_row):
        pl.semaphore_signal(barrier, inc=1, device_id={"row": row_peers[d]}, device_id_type=MESH)
    loaded(pair_ref, gain_ref, qk_ref, vg_ref, mask_ref)
    length = jnp.sum(mask_ref[...].astype(f32), axis=1, keepdims=True)

    half = rows // 2
    col_pos = (iota((1, cols, C), 1) + col_first).astype(f32)
    col_keep = col_pos < length.reshape(1, 1, 1)
    dim_shift = log2(TRI_DIM)
    left = iota((C, C), 0)
    right = iota((C, C), 1)
    same_head = (left >> dim_shift) == (right >> dim_shift)
    key_value_weight = jnp.concatenate([qk_ref[0, :, C:], vg_ref[0, :, :C]], axis=1)
    normed_halves = []
    row_copies = []
    for b in range(2):
        part = pair_ref[b * half:(b + 1) * half].reshape(half * cols, C)
        normed_halves.append(layer_norm(part, gain_ref[0:1, :]).astype(bf16))
        key_value = dot(normed_halves[b], key_value_weight)
        key_feat = jnp.where(col_keep, feature(key_value[:, :C]).reshape(half, cols, C), 0.0).astype(bf16)
        values = key_value[:, C:].astype(bf16).reshape(half, cols, C)
        for i in range(half):
            outer = jnp.where(same_head, dot_tn(key_feat[i], values[i]), 0.0)
            row_part[b * half + i] = jnp.sum(outer.reshape(TRI_HEADS, TRI_DIM, C), axis=0).astype(bf16)
        if b == 0:
            pl.semaphore_wait(barrier, n_row + n_col - 2)
        lines = pl.ds(b * half, half)
        row_copies.append(push_cols(lambda d: row_part.at[lines], lambda d: row_recv.at[d - 1, lines],
                                    row_send_sem.at[b], row_recv_sem.at[b]))

    loaded(single_ref, attn_gain_ref, chain_bias_ref, slope_ref)
    lane = iota((8, C), 1)
    top = iota((8, C), 0) == 0
    relation = jnp.zeros((8, C), f32)
    for h in range(heads_here):
        pick = jnp.where(top, chain_bias_ref[:, h:h + 1], slope_ref[:, h:h + 1])
        relation = relation + jnp.where(lane == my_col * heads_here + h, pick, 0.0)
    rel[my_col] = relation
    rel_copies = push_cols(lambda d: rel.at[my_col], lambda d: rel.at[my_col], rel_send_sem, rel_recv_sem)
    gains = [attn_gain_ref[g:g + 1, :] for g in range(attn_gain_ref.shape[0])]
    tok = layer_norm(single_ref[...], jnp.concatenate(gains, axis=1)).astype(bf16)
    loaded(aqk_ref, avg_ref)
    kv[my_row, 0] = dot_nt(tok, aqk_ref[1]).astype(bf16)
    kv[my_row, 1] = dot_nt(tok, avg_ref[0]).astype(bf16)
    query_gate_weight = jnp.concatenate([qk_ref[0, :, :C], vg_ref[0, :, C:]], axis=1)
    feat_halves = []
    gate_halves = []
    for b in range(2):
        query_gate = dot(normed_halves[b], query_gate_weight)
        feat_halves.append(feature(query_gate[:, :C]).astype(bf16).reshape(half, cols, C))
        gate_halves.append(sigmoid(query_gate[:, C:]) * tri_scale)
    query_gates[my_col, 0] = dot_nt(tok, aqk_ref[0]).astype(bf16)
    query_gates[my_col, 1] = sigmoid(dot_nt(tok, avg_ref[1])).astype(bf16)
    loaded(aout_ref)
    for c in range(n_col):
        aout_send[c] = aout_ref[:, c * width:(c + 1) * width]
    aout_full[my_col] = aout_send[my_col]

    loaded(out_ref, chain_ref, residue_ref, bias_gain_ref, bias_proj_ref)
    key_value_weight = jnp.concatenate([qk_ref[1, :, C:], vg_ref[1, :, :C]], axis=1)
    pairs, normed, key_feat, values = [], [], [], []
    kv_copies = {}
    for b in range(2):
        for copy in row_copies[b]:
            copy.wait_recv()
        if b == 0:
            for d in far_first:
                kv_copies[d] = push(kv.at[my_row], kv.at[my_row], kv_send_sem.at[d - 1],
                                    kv_recv_sem.at[d - 1], {"row": row_peers[d]})
        lines = slice(b * half, (b + 1) * half)
        states = row_part[lines].astype(f32)
        for d in range(1, n_col):
            states = states + row_recv[d - 1, lines].astype(f32)
        states = states.astype(bf16)
        mixed = []
        for i in range(half):
            block = jnp.concatenate([states[i]] * TRI_HEADS, axis=0)
            block = jnp.where(same_head, block, jnp.zeros_like(block))
            mixed.append(dot(feat_halves[b][i], block))
        update = (gate_halves[b] * jnp.concatenate(mixed, axis=0)).astype(bf16)
        part = pair_ref[lines].reshape(half * cols, C).astype(f32)
        pairs.append((part + dot(update, out_ref[0])).astype(bf16))
        normed.append(layer_norm(pairs[b], gain_ref[1:2, :]).astype(bf16))
        key_value = dot(normed[b], key_value_weight)
        row_pos = (iota((half, 1, C), 0) + row_first + b * half).astype(f32)
        row_keep = row_pos < length.reshape(1, 1, 1)
        feat = jnp.where(row_keep, feature(key_value[:, :C]).reshape(half, cols, C), 0.0)
        key_feat.append(feat.astype(bf16).reshape(half * cols, C))
        values.append(key_value[:, C:])
    pair, normed, key_feat, values = [jnp.concatenate(both, axis=0)
                                      for both in (pairs, normed, key_feat, values)]
    qg_copies = push_cols(lambda d: query_gates.at[my_col], lambda d: query_gates.at[my_col],
                          qg_send_sem, qg_recv_sem)

    entry = jnp.where(same_head, left & (TRI_DIM - 1), -1)
    share = TRI_DIM // n_row

    def spread(first, count):
        parts = [(entry == first + s).astype(f32).astype(bf16) for s in range(count)]
        return parts[0] if count == 1 else jnp.concatenate(parts, axis=1)

    rs_copies = {}
    for d in far_first + [0]:
        owner = row_peers[d]
        wide = dot(key_feat, spread(owner * share, share))
        for s in range(share):
            part = wide[:, s * C:(s + 1) * C] * values
            col_part[owner, s] = jnp.sum(part.reshape(rows, cols, C), axis=0).astype(bf16)
        if d:
            rs_copies[d] = push(col_part.at[owner], col_recv.at[d - 1], rs_send_sem.at[d - 1],
                                rs_recv_sem.at[d - 1], {"row": owner})
    for d in far_first:
        kv_copies[d].wait_recv()
    kv_own[my_col] = kv[pl.ds(my_col * per, per)]
    own_copies = push_cols(lambda d: kv.at[pl.ds(col_peers[d] * per, per)], lambda d: kv_own.at[my_col],
                           own_send_sem, own_recv_sem)
    query_gate = dot(normed, jnp.concatenate([qk_ref[1, :, :C], vg_ref[1, :, C:]], axis=1))
    query_feat = feature(query_gate[:, :C]).astype(bf16)
    gate = sigmoid(query_gate[:, C:]) * tri_scale
    for e in range(0, TRI_DIM, 2):
        wide = dot(query_feat, spread(e, 2)).astype(bf16)
        q_wide[e] = wide[:, :C]
        q_wide[e + 1] = wide[:, C:]
    total = col_part[my_row].astype(f32)
    for d in far_first:
        rs_copies[d].wait_recv()
        total = total + col_recv[d - 1].astype(f32)
    col_full[my_row] = total.astype(bf16)
    ag_copies = {}
    for d in far_first:
        ag_copies[d] = push(col_full.at[my_row], col_full.at[my_row], ag_send_sem.at[d - 1],
                            ag_recv_sem.at[d - 1], {"row": row_peers[d]})

    aout_copies = push_cols(lambda d: aout_send.at[col_peers[d]], lambda d: aout_full.at[my_col],
                            aout_send_sem, aout_recv_sem)

    head_shift = log2(heads)
    lines = rows * heads
    for copy in rel_copies + qg_copies + own_copies:
        copy.wait_recv()
    head_of = iota((heads, width), 0)
    head_lane = iota((heads, width), 1)
    lanes_of = []
    for c in range(n_col):
        start = (head_of - c * heads_here) * HEAD_DIM
        lanes_of.append((head_lane >= start) & (head_lane < start + HEAD_DIM))
    scores = jnp.zeros((lines, cols), f32)
    for c in range(n_col):
        query = query_gates[c, 0].astype(f32)
        stack = jnp.where(lanes_of[c][None], query[:, None, :], 0.0).reshape(lines, width).astype(bf16)
        scores = scores + dot_nt(stack, kv_own[c, :, 0].reshape(cols, width))
    scores = scores * (1.0 / math.sqrt(HEAD_DIM))
    here = iota((lines, tokens), 1) == (iota((lines, tokens), 0) >> head_shift) + row_first
    chain = chain_ref[...].astype(f32)
    residue = residue_ref[...]
    my_chain = jnp.sum(jnp.where(here, chain, 0.0), axis=1, keepdims=True)
    my_residue = jnp.sum(jnp.where(here, residue.astype(f32), 0.0), axis=1, keepdims=True)
    relation = rel[0]
    for c in range(1, n_col):
        relation = relation + rel[c]
    own_head = iota((lines, C), 1) == (iota((lines, C), 0) & (heads - 1))
    my_bias = jnp.sum(jnp.where(own_head, relation[0:1], 0.0), axis=1, keepdims=True)
    my_slope = jnp.sum(jnp.where(own_head, relation[1:2], 0.0), axis=1, keepdims=True)
    kind = iota((8, tokens), 0)
    facts = jnp.where(kind == 0, chain, jnp.where(kind == 1, (residue >> 4).astype(f32),
                                                  (residue & 15).astype(f32))).astype(bf16)
    take = (iota((tokens, cols), 0) == iota((tokens, cols), 1) + col_first).astype(f32).astype(bf16)
    facts = dot(facts, take)
    offset = my_residue - (facts[1:2] * 16.0 + facts[2:3])
    offset = jnp.clip(offset, -rel_reach, rel_reach) * (1.0 / rel_reach)
    scores = scores + jnp.where(my_chain == facts[0:1], my_bias + my_slope * offset, 0.0)
    real = (iota((lines, cols), 1) + col_first).astype(f32) < length

    def mix(chunk):
        part = None
        for s in range(share):
            term = (q_wide[chunk * share + s].astype(f32).reshape(rows, cols, C)
                    * col_full[chunk, s].astype(f32).reshape(1, cols, C))
            part = term if part is None else part + term
        return part

    mixed = mix(my_row)
    for d in far_first:
        ag_copies[d].wait_recv()
        mixed = mixed + mix(lax.rem(my_row + n_row - d, n_row))
    update = (gate * mixed.reshape(flat, C)).astype(bf16)
    pair = (pair.astype(f32) + dot(update, out_ref[1])).astype(bf16)
    pair_out_ref[...] = pair.reshape(rows, cols, C)
    store = pltpu.make_async_copy(pair_out_ref, pair_out_hbm, store_sem)
    store.start()

    normed = layer_norm(pair, bias_gain_ref[...]).astype(bf16).reshape(rows, cols, C)
    bias = [dot_nt(bias_proj_ref[...], normed[i]) for i in range(rows)]
    scores = scores + jnp.concatenate(bias, axis=0).astype(bf16).astype(f32)
    weights = jnp.where(real, jnp.exp(cap_value * jnp.tanh(scores * (1.0 / cap_value))), 0.0)
    bottom = jnp.sum(weights, axis=1, keepdims=True)
    weights = weights.astype(bf16)
    lanes = num_send.shape[2]
    spare = lanes - width
    diagonal = iota((heads, spare), 0) == iota((heads, spare), 1)
    bottom = jnp.sum(jnp.where(diagonal[None], bottom.reshape(rows, heads, 1), 0.0), axis=1)
    bottom_high = bottom.astype(bf16).astype(f32)
    extras = [bottom_high, bottom - bottom_high] + [jnp.zeros((rows, spare), f32)] * (n_col - 2)
    tops = []
    for c in range(n_col):
        attended = dot(weights, kv_own[c, :, 1].reshape(cols, width)).reshape(rows, heads, width)
        tops.append(jnp.sum(jnp.where(lanes_of[c][None], attended, 0.0), axis=1))
        num_send[c] = jnp.concatenate([tops[c], extras[c]], axis=1).astype(bf16)
    num_copies = push_cols(lambda d: num_send, lambda d: num_recv.at[d - 1], num_send_sem, num_recv_sem)
    for copy in aout_copies:
        copy.wait_recv()
    deep = iota((spare, width), 0)
    flat_lane = iota((spare, width), 1)
    wide_of = []
    for c in range(n_col):
        start = (deep - c * heads_here) * HEAD_DIM
        wide_of.append(((flat_lane >= start) & (flat_lane < start + HEAD_DIM)).astype(f32).astype(bf16))
    for copy in pushed[:1 - n_col]:
        copy.wait_send()
    for copy in num_copies:
        copy.wait_recv()
    for c in range(n_col):
        for d in range(1, n_col):
            arrived = num_recv[d - 1, c].astype(f32)
            tops[c] = tops[c] + arrived[:, :width]
            if c < 2:
                bottom = bottom + arrived[:, width:]
    inverse = jnp.where(iota((rows, spare), 1) < heads, 1.0 / bottom, 0.0)
    inverse_high = inverse.astype(bf16)
    inverse_low = (inverse - inverse_high.astype(f32)).astype(bf16)
    result = jnp.zeros((rows, width), f32)
    for c in range(n_col):
        factor = query_gates[c, 1].astype(f32) * (dot(inverse_high, wide_of[c]) + dot(inverse_low, wide_of[c]))
        result = result + dot((factor * tops[c]).astype(bf16), aout_full[c])
    token_ref[...] = result.astype(bf16)
    store.wait()
    for copy in pushed[1 - n_col:]:
        copy.wait_send()


def on_device(n_row, n_col, pair_act, single, token_mask, chain_index, residue_index, tri_gain, tri_qk,
              tri_vg, tri_out, bias_gain, bias_proj, chain_bias, pos_slope, attn_gain, attn_qk, attn_vg,
              attn_out):
    rows, cols, _ = pair_act.shape
    width = attn_qk.shape[2]
    share = TRI_DIM // n_row
    per = cols // rows
    lanes = -(-width // C) * C
    by_col = [pltpu.SemaphoreType.DMA((n_col - 1,))] * 2
    by_half = [pltpu.SemaphoreType.DMA((2, n_col - 1))] * 2
    by_row = [pltpu.SemaphoreType.DMA((n_row - 1,))] * 2
    vmem = pl.BlockSpec(memory_space=pltpu.VMEM)
    inputs = (
        pair_act, single, token_mask.reshape(1, -1), chain_index.reshape(1, -1),
        residue_index.reshape(1, -1), tri_gain, tri_qk, tri_vg, tri_out, bias_gain.reshape(1, -1),
        bias_proj.T, chain_bias.reshape(1, -1), pos_slope.reshape(1, -1), attn_gain.reshape(-1, C),
        jnp.swapaxes(attn_qk, 1, 2), jnp.swapaxes(attn_vg, 1, 2), attn_out,
    )
    out_shape = (jax.ShapeDtypeStruct(pair_act.shape, bf16), jax.ShapeDtypeStruct((rows, width), bf16))
    everything = 64 * 1024 * 1024
    return pl.pallas_call(
        functools.partial(kernel, n_row, n_col),
        out_shape=out_shape,
        in_specs=[pl.BlockSpec(memory_space=pltpu.HBM)] * 17,
        out_specs=(pl.BlockSpec(memory_space=pltpu.HBM), vmem),
        scratch_shapes=[pltpu.VMEM(value.shape, value.dtype) for value in inputs[:1] + inputs] + [
            pltpu.VMEM((rows, TRI_DIM, C), bf16),
            pltpu.VMEM((n_col - 1, rows, TRI_DIM, C), bf16),
            pltpu.VMEM((n_row, share, cols, C), bf16),
            pltpu.VMEM((n_row - 1, share, cols, C), bf16),
            pltpu.VMEM((n_row, share, cols, C), bf16),
            pltpu.VMEM((TRI_DIM, rows * cols, C), bf16),
            pltpu.VMEM((n_row, 2, rows, width), bf16),
            pltpu.VMEM((n_col, per, 2, rows, width), bf16),
            pltpu.VMEM((n_col, 2, rows, width), bf16),
            pltpu.VMEM((n_col, 8, C), f32),
            pltpu.VMEM((n_col, width, width), bf16),
            pltpu.VMEM((n_col, width, width), bf16),
            pltpu.VMEM((n_col, rows, lanes), bf16),
            pltpu.VMEM((n_col - 1, n_col, rows, lanes), bf16),
            pltpu.SemaphoreType.DMA((len(inputs),)),
            pltpu.SemaphoreType.DMA,
        ] + by_half + by_row + by_row + by_row + by_col * 5,
        compiler_params=pltpu.CompilerParams(
            collective_id=0, has_side_effects=True, vmem_limit_bytes=everything
        ),
    )(*inputs)


def solution(mesh):
    return jax.shard_map(
        functools.partial(on_device, mesh.shape["row"], mesh.shape["col"]),
        mesh=mesh,
        in_specs=(
            P(("grp", "row"), "col", None),
            P(("grp", "row"), None),
            P("grp"),
            P("grp"),
            P("grp"),
            P(),
            P(),
            P(),
            P(),
            P(),
            P(),
            P("col"),
            P("col"),
            P(),
            P(None, None, "col"),
            P(None, None, "col"),
            P("col", None),
        ),
        out_specs=(P(("grp", "row"), "col", None), P(("grp", "row"), "col")),
        check_vma=False,
    )
```
